128 devices in a mesh: group: 16 (over y, z), member: 8 (over x, core).
Axes of the slice: x: 4, y: 4, z: 4, core: 2. Of those that a mesh axis runs over, the one named last changes fastest.
Arguments:
- embed: bfloat16 [65536, 768], P(('group', 'member'))
- destination: int32 [65536], P(('group', 'member')), may hold values from 0 to 127, as said below
- cluster: int32 [65536], P(('group', 'member')), may hold values from 0 to 3
Outputs:
- dupscore: float32 [65536], P(('group', 'member'))
The draws below stay inside these ranges and needn't reach their ends.
Inputs may be any that keep to these rules, and one draw needn't show every extreme that they name: Among the rows of one device at most 8 name the same destination, and there is one destination device (which varies by draw) that receives exactly 8 rows from every device.
All inputs are finite; a program needn't handle non-finite values.
Results may differ from the reference program's by a relative error of at most 0.00065.
Values may be sent and summed in bfloat16 or wider, within the bound.
A program may use at most 64 MiB of HBM per device.

```python
import jax
import jax.numpy as jnp
from jax import lax

D = 768
ROW_DEV = 512
CL_GROUP = 4
PAIR = 8
N_GROUP = 16
N_MEMBER = 8


def routing(key):
    devices = N_GROUP * N_MEMBER
    slot_total = devices * PAIR
    key_heavy, key_jitter, key_chosen, key_shuffle, key_cluster = jax.random.split(key, 5)
    slot_dest = jnp.arange(slot_total, dtype=jnp.int32) // PAIR
    slot_first = jnp.arange(slot_total, dtype=jnp.int32) % PAIR == 0
    source_dev = jnp.arange(devices, dtype=jnp.int32)
    reach = min(devices, ROW_DEV // 2)
    covered = ((slot_dest[None, :] - source_dev[:, None]) % devices < reach) & slot_first[None, :]
    group_heavy = jax.random.randint(key_heavy, (N_GROUP,), 0, 4)
    jitter_draw = jax.random.randint(key_jitter, (devices, slot_total), 0, 2048)
    chosen = jax.random.randint(key_chosen, (), 0, devices)
    slot_score = jitter_draw + group_heavy[slot_dest // N_MEMBER][None, :] * 1024 + covered.astype(jnp.int32) * 4096 + (slot_dest == chosen).astype(jnp.int32)[None, :] * 8192
    order_key = slot_score * slot_total + jnp.arange(slot_total, dtype=jnp.int32)[None, :]
    ignored, picked = lax.top_k(order_key, ROW_DEV)
    target_dev = (picked // PAIR).astype(jnp.int32)
    shuffle_key = jax.random.randint(key_shuffle, (devices, ROW_DEV), 0, 2 ** 20) * ROW_DEV + jnp.arange(ROW_DEV, dtype=jnp.int32)[None, :]
    shuffle = jnp.argsort(shuffle_key, axis=1)
    target_dev = jnp.take_along_axis(target_dev, shuffle, axis=1).reshape(-1)
    subcluster = jax.random.randint(key_cluster, (devices * ROW_DEV,), 0, CL_GROUP)
    return (target_dev.astype(jnp.int32), subcluster.astype(jnp.int32))


def draw_destination(key, part):
    target_dev, subcluster = routing(key)
    return target_dev


def draw_cluster(key, part):
    target_dev, subcluster = routing(key)
    return subcluster


def draw_embed(key, part):
    target_dev, subcluster = routing(key)
    key = jax.random.fold_in(key, 7)
    row_total = target_dev.shape[0]
    team_label = target_dev // N_MEMBER
    per_cluster = max(1, ROW_DEV * N_MEMBER // (CL_GROUP * 8))
    per_team = per_cluster * CL_GROUP
    key_family, key_center, key_vector, key_weight, key_jitter, key_column, key_row = jax.random.split(key, 7)
    family = team_label * per_team + jax.random.randint(key_family, (row_total,), 0, per_team)
    centers = jax.vmap(lambda team_id: jax.random.normal(jax.random.fold_in(key_center, team_id), (D,), jnp.float32))(team_label)
    vectors = jax.vmap(lambda family_id: jax.random.normal(jax.random.fold_in(key_vector, family_id), (D,), jnp.float32))(family)
    weight = jax.random.uniform(key_weight, (row_total, 1), jnp.float32, 0.3, 1.6)
    column_scale = jnp.exp(jax.random.uniform(key_column, (D,), jnp.float32, jnp.log(0.3), jnp.log(3.0)))
    jitter_draw = jax.random.normal(key_jitter, (row_total, D), jnp.float32)
    row_scale = jnp.exp(jax.random.uniform(key_row, (row_total, 1), jnp.float32, 0.0, jnp.log(10.0)))
    mixed = (0.6 * centers + weight * vectors + jitter_draw) * column_scale[None, :] * row_scale
    return mixed.astype(jnp.bfloat16)


def setup_inputs(seed: int = 0) -> dict:
    arg_keys = jax.random.split(jax.random.key(seed), 4)
    return {
        "embed": draw_embed(jax.random.fold_in(arg_keys[3], 71), 0),
        "destination": draw_destination(jax.random.fold_in(arg_keys[3], 71), 0),
        "cluster": draw_cluster(jax.random.fold_in(arg_keys[3], 71), 0),
    }


def pick_block(row_total):
    for block_size in (512, 256, 128):
        if row_total % block_size == 0:
            return block_size
    return row_total

def reference(embed, destination, cluster):
    values = embed.astype(jnp.float32)
    unit_rows = (values * lax.rsqrt(lax.optimization_barrier(jnp.sum(values * values, axis=1, keepdims=True)) + 1e-06)).astype(jnp.bfloat16)
    team_index = (destination // N_MEMBER).astype(jnp.int32)
    row_total = unit_rows.shape[0]
    capacity = N_MEMBER * N_GROUP * N_MEMBER * PAIR
    block_size = pick_block(capacity)
    columns = jnp.arange(capacity, dtype=jnp.int32)

    def per_group(group_index):
        inside = team_index == group_index
        member_ids = jnp.nonzero(inside, size=capacity, fill_value=0)[0].astype(jnp.int32)
        fill_count = jnp.sum(inside.astype(jnp.int32))
        filled = columns < fill_count
        vectors = unit_rows[member_ids]
        labels = jnp.where(filled, cluster[member_ids], -1).astype(jnp.int32)

        def one_block(offset):
            left_rows = lax.dynamic_slice_in_dim(vectors, offset, block_size, 0)
            left_labels = lax.dynamic_slice_in_dim(labels, offset, block_size, 0)
            similar = jnp.dot(left_rows, vectors.T, preferred_element_type=jnp.float32)
            places = offset + jnp.arange(block_size, dtype=jnp.int32)
            allowed = (left_labels[:, None] == labels[None, :]) & (left_labels[:, None] >= 0) & (places[:, None] != columns[None, :])
            return lax.optimization_barrier(jnp.max(jnp.where(allowed, similar, -2.0), axis=1))
        offsets = jnp.arange(capacity // block_size, dtype=jnp.int32) * block_size
        best_match = lax.map(one_block, offsets).reshape(-1)
        return (member_ids, filled, best_match)
    member_ids, filled, best_match = lax.map(per_group, jnp.arange(N_GROUP, dtype=jnp.int32))
    target_rows = jnp.where(filled, member_ids, row_total).reshape(-1)
    scores = jnp.maximum(best_match, -1.0).reshape(-1)
    dupscore = jnp.full((row_total,), -1.0, jnp.float32).at[target_rows].set(scores, mode='drop')
    return dupscore
```

```python
import jax
import jax.numpy as jnp
from jax import lax
from jax.experimental import pallas as pl
from jax.experimental.pallas import tpu as pltpu
from jax.sharding import PartitionSpec as P

MESH = pl.DeviceIdType.MESH
SIDE = 4
CELLS = 64
CELL = 16
SPILL = 80
LANES = 128
SLOTS = CELLS * CELL
FORWARD = 3 * SPILL
LEFT_SPILL = 256
NONE = -4.0
FAILED = 8.0
EMPTY = 2.0


def split3(value):
    high = value.astype(jnp.bfloat16)
    rest = value - high.astype(jnp.float32)
    mid = rest.astype(jnp.bfloat16)
    low = (rest - mid.astype(jnp.float32)).astype(jnp.bfloat16)
    return high, mid, low


def iota(shape, dim):
    return lax.broadcasted_iota(jnp.int32, shape, dim)


def dot(left, right):
    return jnp.dot(left, right, preferred_element_type=jnp.float32)


def dot_t(left, right):
    return lax.dot_general(left, right, (((1,), (1,)), ((), ())), preferred_element_type=jnp.float32)


def fold(scores):
    rows, columns = scores.shape
    return jnp.max(scores.reshape(rows // 8, 8, columns), axis=0)


def team_kernel(
    embed_ref,
    dest_ref,
    cluster_ref,
    out_ref,
    unit,
    send,
    meta,
    left,
    meta_in,
    other,
    other_spill,
    select,
    forward,
    label_out,
    label_in,
    bias,
    other_bias,
    spill_best,
    spill_ret,
    best_out,
    best_in,
    line_sem,
    plane_sem,
    send_sems,
    recv_sems,
    meta_sem,
    pair_sems,
    spill_sems,
    ret_sems,
    best_sem,
    own_sems,
):
    group = lax.axis_index("group")
    member = lax.axis_index("member")
    y, z = group // SIDE, group % SIDE
    x, core = member // 2, member % 2
    me = group * SIDE + x

    def at(dy, dz, dx, dcore=0):
        yy, zz, xx = (y + dy) % SIDE, (z + dz) % SIDE, (x + dx) % SIDE
        cell = (yy * SIDE + zz) * SIDE + xx
        return cell, {"group": yy * SIDE + zz, "member": xx * 2 + (core + dcore) % 2}

    def step(index):
        return at(index // 16, (index // 4) % 4, index % 4)

    barrier = pltpu.get_barrier_semaphore()
    for d in range(1, SIDE):
        for offset in ((d, 0, 0), (0, d, 0), (0, 0, d)):
            pl.semaphore_signal(barrier, inc=1, device_id=at(*offset)[1], device_id_type=MESH)
    sibling = at(0, 0, 0, 1)[1]
    pl.semaphore_signal(barrier, inc=1, device_id=sibling, device_id_type=MESH)

    values = embed_ref[...].astype(jnp.float32)
    norm = jnp.sum(values * values, axis=1, keepdims=True)
    unit[...] = (values * lax.rsqrt(norm + 1e-06)).astype(jnp.bfloat16)

    pl.semaphore_wait(barrier, 10)
    for d in range(1, SIDE):
        pl.semaphore_signal(line_sem, inc=1, device_id=at(0, d, 0)[1], device_id_type=MESH)

    rows = dest_ref.shape[1]
    team = lax.shift_right_logical(dest_ref[...], 3)
    cluster = cluster_ref[...]
    in_team = (iota((16, rows), 0) == team).astype(jnp.float32)
    cells = jnp.concatenate(
        [in_team * (cluster == c).astype(jnp.float32) for c in range(4)], axis=0
    )
    earlier = (iota((rows, rows), 0) < iota((rows, rows), 1)).astype(jnp.bfloat16)
    rank = jnp.sum(cells * dot(cells.astype(jnp.bfloat16), earlier), axis=0, keepdims=True)
    counts = jnp.minimum(jnp.sum(cells, axis=1, keepdims=True), float(CELL))
    over = rank >= float(CELL)
    over_team = in_team * over.astype(jnp.float32)
    order = jnp.sum(
        over_team * dot(over_team.astype(jnp.bfloat16), earlier), axis=0, keepdims=True
    )
    filled = [
        jnp.sum(in_team * counts[16 * c : 16 * c + 16], axis=0, keepdims=True) for c in range(4)
    ]
    free0 = CELL - filled[0]
    free1 = free0 + CELL - filled[1]
    free2 = free1 + CELL - filled[2]
    chip = (
        (order >= free0).astype(jnp.int32)
        + (order >= free1).astype(jnp.int32)
        + (order >= free2).astype(jnp.int32)
    )
    place = jnp.where(
        chip == 0,
        filled[0] + order,
        jnp.where(
            chip == 1,
            filled[1] + order - free0,
            jnp.where(chip == 2, filled[2] + order - free1, filled[3] + order - free2),
        ),
    )
    chip = jnp.where(over, chip, cluster)
    place = jnp.where(over, place, rank).astype(jnp.int32)
    cell = team * 4 + chip
    slot = cell * CELL + place
    lane = place + (me % 8) * CELL

    pl.semaphore_wait(line_sem, 3)
    for d in range(1, SIDE):
        pl.semaphore_signal(plane_sem, inc=1, device_id=at(0, 0, d)[1], device_id_type=MESH)

    in_cell = (iota((CELLS, rows), 0) == cell).astype(jnp.float32)
    at_lane = (iota((LANES, rows), 0) == lane).astype(jnp.bfloat16)
    labels = (in_cell * (cluster + 1).astype(jnp.float32)).astype(jnp.bfloat16)
    meta[...] = dot_t(labels, at_lane).reshape(CELLS, 1, LANES)

    def pack(index, carry):
        base = pl.multiple_of(index * 256, 256)
        chosen = (iota((256, rows), 0) + base == slot).astype(jnp.bfloat16)
        send[pl.ds(base, 256)] = dot(chosen, unit[...]).astype(jnp.bfloat16)
        return carry

    lax.fori_loop(0, SLOTS // 256, pack, 0)
    pl.semaphore_wait(plane_sem, 3)

    def cell_rows(ref, index):
        return ref.at[pl.ds(pl.multiple_of(index * CELL, CELL), CELL)]

    def send_cell(index, carry):
        target, device = step((index * 37) % CELLS)
        pltpu.make_async_remote_copy(
            src_ref=cell_rows(send, target),
            dst_ref=cell_rows(left, me),
            send_sem=send_sems.at[0],
            recv_sem=recv_sems.at[y],
            device_id=device,
            device_id_type=MESH,
        ).start()
        pltpu.make_async_remote_copy(
            src_ref=meta.at[pl.ds(target, 1)],
            dst_ref=meta_in.at[pl.ds(me, 1)],
            send_sem=send_sems.at[1],
            recv_sem=meta_sem,
            device_id=device,
            device_id_type=MESH,
        ).start()
        return carry

    lax.fori_loop(1, CELLS, send_cell, 0)
    pltpu.make_async_copy(cell_rows(send, me), cell_rows(left, me), recv_sems.at[y]).start()
    pltpu.make_async_copy(
        meta.at[pl.ds(me, 1)], meta_in.at[pl.ds(me, 1)], meta_sem
    ).start()
    left[SLOTS + FORWARD :] = jnp.zeros((LEFT_SPILL - FORWARD, left.shape[1]), jnp.bfloat16)

    pltpu.make_async_copy(meta_in, meta_in, meta_sem).wait()
    to_pair = []
    for q in range(4):
        part = pl.ds(q * 256, 256)
        pltpu.make_async_copy(left.at[part], left.at[part], recv_sems.at[q]).wait()
        copy = pltpu.make_async_remote_copy(
            src_ref=left.at[part],
            dst_ref=other.at[part],
            send_sem=pair_sems.at[0, q],
            recv_sem=pair_sems.at[1, q],
            device_id=sibling,
            device_id_type=MESH,
        )
        copy.start()
        to_pair.append(copy)

    label = jnp.sum(meta_in[...].reshape(8, 8, LANES), axis=1)
    own = (x + 1).astype(jnp.float32)
    below = (iota((LANES, LANES), 0) < iota((LANES, LANES), 1)).astype(jnp.bfloat16)
    hits = [
        (label == (lax.rem(x + d, SIDE) + 1).astype(jnp.float32)).astype(jnp.float32)
        for d in range(1, SIDE)
    ]
    hit = jnp.concatenate(hits, axis=0)
    within = dot(hit.astype(jnp.bfloat16), below)
    totals = jnp.sum(hit, axis=1, keepdims=True)
    places = jnp.full((8, LANES), -1.0, jnp.float32)
    worst = jnp.zeros((1, 1), jnp.float32)
    for d in range(3):
        total = totals[8 * d : 8 * d + 8]
        before = jnp.sum(
            jnp.where(
                iota((8, 8), 0) < iota((8, 8), 1),
                jnp.broadcast_to(total, (8, 8)),
                0.0,
            ),
            axis=0,
            keepdims=True,
        )
        spread = jnp.sum(
            jnp.where(iota((8, 8), 0) == iota((8, 8), 1), jnp.broadcast_to(before, (8, 8)), 0.0),
            axis=1,
            keepdims=True,
        )
        position = within[8 * d : 8 * d + 8] + spread
        places = jnp.where(
            (hits[d] > 0.0) & (position < float(SPILL)), position + float(SPILL * d), places
        )
        worst = jnp.maximum(worst, jnp.sum(total, axis=0, keepdims=True))
    failed = jnp.broadcast_to((worst > float(SPILL)).astype(jnp.float32), (8, LANES))
    for q in range(8):
        select[:, q * LANES : (q + 1) * LANES] = (
            iota((LEFT_SPILL, LANES), 0).astype(jnp.float32) == places[q : q + 1]
        ).astype(jnp.bfloat16)
    chosen = select[0:FORWARD]
    taken = jnp.sum(chosen.astype(jnp.float32), axis=1, keepdims=True)
    moved = dot(chosen, left[0:SLOTS])
    mark = jnp.where((iota((FORWARD, LANES), 1) == 0) & (taken < 0.5), EMPTY, 0.0)
    forward[:, 0:LANES] = (moved[:, 0:LANES] + mark).astype(jnp.bfloat16)
    forward[:, LANES:] = moved[:, LANES:].astype(jnp.bfloat16)
    to_line = []
    for d in range(3):
        copy = pltpu.make_async_remote_copy(
            src_ref=forward.at[pl.ds(d * SPILL, SPILL)],
            dst_ref=left.at[pl.ds(SLOTS + d * SPILL, SPILL)],
            send_sem=spill_sems.at[0, d],
            recv_sem=spill_sems.at[1, d],
            device_id=at(0, 0, d + 1)[1],
            device_id_type=MESH,
        )
        copy.start()
        to_line.append(copy)
    label_out[0:8] = label
    label_out[8:16] = failed
    copy_label = pltpu.make_async_remote_copy(
        src_ref=label_out,
        dst_ref=label_in,
        send_sem=pair_sems.at[0, 4],
        recv_sem=pair_sems.at[1, 4],
        device_id=sibling,
        device_id_type=MESH,
    )
    copy_label.start()

    def set_bias(ref, tags):
        columns = jnp.transpose(tags)
        for q in range(8):
            ref[q * LANES : (q + 1) * LANES, 0:1] = jnp.where(
                columns[:, q : q + 1] == own, 0.0, NONE
            )

    def against(right, right_bias, first, count, same):
        def one(index, best):
            base = pl.multiple_of(index * 256, 256)
            part = pl.ds(base, 256)
            scores = dot_t(right[part], left[first : first + count]) + right_bias[part, 0:1]
            if same:
                scores = jnp.where(
                    iota((256, count), 0) + base == iota((256, count), 1), NONE, scores
                )
            return jnp.maximum(best, fold(scores))

        start = jnp.full((8, count), NONE, jnp.float32)
        return lax.fori_loop(0, SLOTS // 256, one, start)

    set_bias(bias, label)
    best_main = against(left, bias, 0, SLOTS, True)
    copy_label.wait()
    set_bias(other_bias, label_in[0:8])
    for copy in to_pair:
        copy.wait()
    best_main = jnp.maximum(best_main, against(other, other_bias, 0, SLOTS, False))

    for copy in to_line:
        copy.wait()
    spill_part = pl.ds(SLOTS, FORWARD)
    spill_pair = pltpu.make_async_remote_copy(
        src_ref=left.at[spill_part],
        dst_ref=other_spill,
        send_sem=pair_sems.at[0, 5],
        recv_sem=pair_sems.at[1, 5],
        device_id=sibling,
        device_id_type=MESH,
    )
    spill_pair.start()
    best_spill = against(left, bias, SLOTS, LEFT_SPILL, False)
    best_spill = jnp.maximum(best_spill, against(other, other_bias, SLOTS, LEFT_SPILL, False))

    def against_spill(right, same):
        scores = dot_t(right, left[...]) + jnp.where(
            right[:, 0:1].astype(jnp.float32) > 1.5, NONE, 0.0
        )
        if same:
            scores = jnp.where(
                iota(scores.shape, 0) + SLOTS == iota(scores.shape, 1), NONE, scores
            )
        return fold(scores)

    best_all = against_spill(left[SLOTS : SLOTS + FORWARD], True)
    spill_pair.wait()
    best_all = jnp.maximum(best_all, against_spill(other_spill[...], False))
    best_main = jnp.maximum(best_main, best_all[:, 0:SLOTS])
    best_spill = jnp.maximum(best_spill, best_all[:, SLOTS:])
    spill_best[...] = jnp.max(best_spill, axis=0, keepdims=True)

    back = []
    for d in range(3):
        copy = pltpu.make_async_remote_copy(
            src_ref=spill_best,
            dst_ref=spill_ret.at[d],
            send_sem=ret_sems.at[0, d],
            recv_sem=ret_sems.at[1, d],
            device_id=at(0, 0, 3 - d)[1],
            device_id_type=MESH,
        )
        copy.start()
        back.append(copy)
    best_row = jnp.max(best_main, axis=0, keepdims=True)
    failed = jnp.maximum(failed, label_in[8:16])
    for copy in back:
        copy.wait()
    returned = jnp.zeros((1, LEFT_SPILL), jnp.float32)
    spot = iota((1, LEFT_SPILL), 1)
    for d in range(3):
        returned = jnp.where(
            (spot >= SPILL * d) & (spot < SPILL * (d + 1)), spill_ret[d], returned
        )
    stacked = jnp.zeros((16, LEFT_SPILL), jnp.float32)
    for index, piece in enumerate(split3(returned)):
        stacked = jnp.where(iota((16, LEFT_SPILL), 0) == index, piece.astype(jnp.float32), stacked)
    moved_best = jnp.sum(dot(stacked.astype(jnp.bfloat16), select[...]), axis=0, keepdims=True)
    for q in range(8):
        part = slice(q * LANES, (q + 1) * LANES)
        row = jnp.where(label[q : q + 1] == own, best_row[:, part], moved_best[:, part])
        best_out[q] = jnp.where(failed[0:1] > 0.0, FAILED, row)

    def send_best(index, carry):
        target, device = step((index * 37) % CELLS)
        pltpu.make_async_remote_copy(
            src_ref=best_out.at[pl.ds(target // 8, 1)],
            dst_ref=best_in.at[pl.ds(me, 1)],
            send_sem=send_sems.at[2],
            recv_sem=best_sem,
            device_id=device,
            device_id_type=MESH,
        ).start()
        return carry

    lax.fori_loop(1, CELLS, send_best, 0)
    pltpu.make_async_copy(
        best_out.at[pl.ds(me // 8, 1)], best_in.at[pl.ds(me, 1)], best_sem
    ).start()
    pltpu.make_async_copy(best_in, best_in, best_sem).wait()

    found = best_in[...].reshape(CELLS, LANES)
    worst = jnp.max(jnp.max(found, axis=1, keepdims=True), axis=0, keepdims=True)
    picked = sum(dot(piece, at_lane) for piece in split3(found))
    score = jnp.maximum(jnp.sum(picked * in_cell, axis=0, keepdims=True), -1.0)
    out_ref[...] = jnp.where(worst > 4.0, FAILED, score)

    sent = pl.ds(0, SLOTS - CELL)
    pltpu.make_async_copy(send.at[sent], send.at[sent], send_sems.at[0]).wait()
    sent = pl.ds(0, CELLS - 1)
    pltpu.make_async_copy(meta.at[sent], meta.at[sent], send_sems.at[1]).wait()
    pltpu.make_async_copy(best_in.at[sent], best_in.at[sent], send_sems.at[2]).wait()


def team_scores(embed, destination, cluster):
    rows, features = embed.shape
    bf16, f32 = jnp.bfloat16, jnp.float32
    vmem = pl.BlockSpec(memory_space=pltpu.VMEM)
    dma = pltpu.SemaphoreType.DMA
    return pl.pallas_call(
        team_kernel,
        out_shape=jax.ShapeDtypeStruct((1, rows), f32),
        in_specs=[vmem] * 3,
        out_specs=vmem,
        scratch_shapes=[
            pltpu.VMEM((rows, features), bf16),
            pltpu.VMEM((SLOTS, features), bf16),
            pltpu.VMEM((CELLS, 1, LANES), f32),
            pltpu.VMEM((SLOTS + LEFT_SPILL, features), bf16),
            pltpu.VMEM((CELLS, 1, LANES), f32),
            pltpu.VMEM((SLOTS, features), bf16),
            pltpu.VMEM((FORWARD, features), bf16),
            pltpu.VMEM((LEFT_SPILL, SLOTS), bf16),
            pltpu.VMEM((FORWARD, features), bf16),
            pltpu.VMEM((16, LANES), f32),
            pltpu.VMEM((16, LANES), f32),
            pltpu.VMEM((SLOTS, LANES), f32),
            pltpu.VMEM((SLOTS, LANES), f32),
            pltpu.VMEM((1, LEFT_SPILL), f32),
            pltpu.VMEM((3, 1, LEFT_SPILL), f32),
            pltpu.VMEM((8, 1, LANES), f32),
            pltpu.VMEM((CELLS, 1, LANES), f32),
            pltpu.SemaphoreType.REGULAR,
            pltpu.SemaphoreType.REGULAR,
            dma((3,)),
            dma((4,)),
            dma,
            dma((2, 6)),
            dma((2, 3)),
            dma((2, 3)),
            dma,
            dma((2,)),
        ],
        compiler_params=pltpu.CompilerParams(
            collective_id=0, has_side_effects=True, vmem_limit_bytes=40 * 2**20
        ),
        name="team_scores",
    )(embed, destination.reshape(1, rows), cluster.reshape(1, rows))


def pick_block(row_total):
    for block_size in (512, 256, 128):
        return block_size
    return row_total


def tile_best(left_rows, left_labels, left_slots, right_rows, right_labels, right_slots):
    row_total = left_rows.shape[0]
    right_total = right_rows.shape[0]
    block_size = pick_block(row_total)
    col_size = pick_block(right_total)
    col_count = right_total // col_size
    right_tiles = right_rows.reshape(col_count, col_size, right_rows.shape[1])
    right_tags = right_labels.reshape(col_count, col_size)
    right_places = right_slots.reshape(col_count, col_size)
    right_low = jnp.min(jnp.where(right_tags >= 0, right_tags, 2**30), axis=1)
    right_high = jnp.max(right_tags, axis=1)

    def one_block(offset):
        piece_rows = lax.dynamic_slice_in_dim(left_rows, offset, block_size, 0)
        piece_labels = lax.dynamic_slice_in_dim(left_labels, offset, block_size, 0)
        piece_slots = lax.dynamic_slice_in_dim(left_slots, offset, block_size, 0)
        left_low = jnp.min(jnp.where(piece_labels >= 0, piece_labels, 2**30))
        left_high = jnp.max(piece_labels)

        def one_column(carry, items):
            tile_rows, tile_labels, tile_slots, low_bound, high_bound = items

            def compute(unused):
                similar = lax.dot_general(
                    piece_rows,
                    tile_rows,
                    (((1,), (1,)), ((), ())),
                    preferred_element_type=jnp.float32,
                )
                allowed = (
                    (piece_labels[:, None] == tile_labels[None, :])
                    & (piece_labels[:, None] >= 0)
                    & (piece_slots[:, None] != tile_slots[None, :])
                )
                masked = jnp.where(allowed, similar, -2.0)
                return (jnp.max(masked, axis=1), jnp.max(masked, axis=0))

            def skipped(unused):
                return (
                    jnp.full((block_size,), -2.0, jnp.float32),
                    jnp.full((col_size,), -2.0, jnp.float32),
                )

            meets = (low_bound <= left_high) & (left_low <= high_bound)
            row_part, col_part = lax.cond(meets, compute, skipped, 0)
            return (jnp.maximum(carry, row_part), col_part)

        row_part, col_parts = lax.scan(
            one_column,
            jnp.full((block_size,), -2.0, jnp.float32),
            (right_tiles, right_tags, right_places, right_low, right_high),
        )
        return (row_part, col_parts.reshape(-1))

    offsets = jnp.arange(row_total // block_size, dtype=jnp.int32) * block_size
    row_best, col_best = lax.map(one_block, offsets)
    return (row_best.reshape(-1), jnp.max(col_best, axis=0))


def general(embed, destination, cluster):
    devices = lax.axis_size(("group", "member"))
    row_total = embed.shape[0]
    feature_dim = embed.shape[1]
    per_pair = max(2, 2 * row_total // devices)
    capacity = devices * per_pair
    values = embed.astype(jnp.float32)
    unit_rows = (
        values * lax.rsqrt(jnp.sum(values * values, axis=1, keepdims=True) + 1e-06)
    ).astype(jnp.bfloat16)
    dest_hits = (destination[:, None] == jnp.arange(devices, dtype=jnp.int32)[None, :]).astype(
        jnp.int32
    )
    before = jnp.cumsum(dest_hits, axis=0) - dest_hits
    rank_index = jnp.sum(before * dest_hits, axis=1)
    slot_index = destination * per_pair + rank_index
    outgoing = jnp.zeros((capacity, feature_dim), jnp.bfloat16).at[slot_index].set(unit_rows)
    out_labels = jnp.full((capacity,), -1, jnp.int32).at[slot_index].set(cluster)
    position = lax.axis_index("member")
    own_base = position * capacity
    arrived, arrived_labels = (
        lax.all_to_all(
            outgoing.reshape(devices, per_pair, feature_dim),
            ("group", "member"),
            split_axis=0,
            concat_axis=0,
            tiled=True,
        ),
        lax.all_to_all(
            out_labels.reshape(devices, per_pair),
            ("group", "member"),
            split_axis=0,
            concat_axis=0,
            tiled=True,
        ),
    )
    plain_block = arrived.reshape(capacity, feature_dim)
    plain_labels = arrived_labels.reshape(capacity)
    slot_order = jnp.arange(capacity, dtype=jnp.int32)
    sort_key = jnp.where(plain_labels >= 0, plain_labels, 2**20) * capacity + slot_order
    order = jnp.argsort(sort_key)
    own_block = plain_block[order]
    own_labels = plain_labels[order]
    own_slots = own_base + order
    row_best, ignored = tile_best(
        own_block,
        own_labels,
        own_slots,
        lax.all_gather(own_block, "member", axis=0, tiled=True),
        lax.all_gather(own_labels, "member", axis=0, tiled=True),
        lax.all_gather(own_slots, "member", axis=0, tiled=True),
    )
    best_match = jnp.maximum(jnp.full((capacity,), -2.0, jnp.float32), row_best)
    sorted_scores = jnp.maximum(best_match, -1.0)
    scores = jnp.zeros((capacity,), jnp.float32).at[order].set(sorted_scores)
    returned_scores = lax.all_to_all(
        scores.reshape(devices, per_pair),
        ("group", "member"),
        split_axis=0,
        concat_axis=0,
        tiled=True,
    )
    return returned_scores.reshape(capacity)[slot_index]


def shards(embed, destination, cluster):
    rows = embed.shape[0]
    scores = team_scores(embed, destination, cluster)
    return lax.cond(
        scores[0, 0] > 4.0,
        general,
        lambda *unused: scores.reshape(rows),
        embed,
        destination,
        cluster,
    )


def solution(mesh):
    in_specs = (P(("group", "member"), None), P(("group", "member")), P(("group", "member")))
    out_specs = P(("group", "member"))
    return jax.shard_map(shards, mesh=mesh, in_specs=in_specs, out_specs=out_specs, check_vma=False)
```

```python
import functools
import types

import jax
import jax.numpy as jnp
from jax import lax
from jax.experimental import pallas as pl
from jax.experimental.pallas import tpu as pltpu
from jax.sharding import PartitionSpec as P

MESH = pl.DeviceIdType.MESH
SIDE = 4
CELLS = 64
CELL = 16
SPILL = 80
LANES = 128
QUARTER = 256
SLOTS = CELLS * CELL
FORWARD = 3 * SPILL
LEFT_SPILL = 256
NONE = -4.0
FAILED = 8.0
EMPTY = 2.0


def split3(value):
    high = value.astype(jnp.bfloat16)
    rest = value - high.astype(jnp.float32)
    mid = rest.astype(jnp.bfloat16)
    low = (rest - mid.astype(jnp.float32)).astype(jnp.bfloat16)
    return high, mid, low


def iota(shape, dim):
    return lax.broadcasted_iota(jnp.int32, shape, dim)


def dot(left, right):
    return jnp.dot(left, right, preferred_element_type=jnp.float32)


def dot_t(left, right):
    return lax.dot_general(left, right, (((1,), (1,)), ((), ())), preferred_element_type=jnp.float32)


def fold(scores):
    rows, columns = scores.shape
    return jnp.max(scores.reshape(rows // 8, 8, columns), axis=0)


def column(tags, index):
    return jnp.transpose(tags)[:, index : index + 1]


class Place:
    def __init__(self):
        group = lax.axis_index("group")
        member = lax.axis_index("member")
        self.y, self.z = group // SIDE, group % SIDE
        self.x, self.core = member // 2, member % 2
        self.cell = group * SIDE + self.x
        self.sum = (self.y + self.z + self.x) % SIDE
        self.source = self.sum * 16 + self.y * SIDE + self.z
        self.sibling = self.at(0, 0, 0, 1)[2]

    def at(self, dy, dz, dx, dcore=0):
        y, z, x = (self.y + dy) % SIDE, (self.z + dz) % SIDE, (self.x + dx) % SIDE
        plane = y * SIDE + z
        source = ((y + z + x) % SIDE) * 16 + plane
        device = {"group": plane, "member": x * 2 + (self.core + dcore) % 2}
        return plane * SIDE + x, source, device

    def offset(self, phase, index):
        dy, dz = index // SIDE, index % SIDE
        return self.at(dy, dz, (phase + 8 - dy - dz) % SIDE)


def wait_for(ref, sem):
    pltpu.make_async_copy(ref, ref, sem).wait()


def greet(place, s):
    barrier = pltpu.get_barrier_semaphore()
    for d in range(1, SIDE):
        for offset in ((d, 0, 0), (0, d, 0), (0, 0, d)):
            device = place.at(*offset)[2]
            pl.semaphore_signal(barrier, inc=1, device_id=device, device_id_type=MESH)
    pl.semaphore_signal(barrier, inc=1, device_id=place.sibling, device_id_type=MESH)
    return barrier


def regroup(place, s):
    load = [
        pltpu.make_async_copy(src, dst, s.load_sems.at[n])
        for n, (src, dst) in enumerate(
            ((s.dest_hbm, s.dest), (s.cluster_hbm, s.cluster), (s.embed_hbm, s.embed))
        )
    ]
    for copy in load:
        copy.start()
    barrier = greet(place, s)
    load[0].wait()
    load[1].wait()

    rows = s.dest.shape[1]
    team = lax.shift_right_logical(s.dest[...], 3)
    cluster = s.cluster[...]
    in_team = (iota((16, rows), 0) == team).astype(jnp.float32)
    cells = jnp.concatenate(
        [in_team * (cluster == c).astype(jnp.float32) for c in range(4)], axis=0
    )
    earlier = (iota((rows, rows), 0) < iota((rows, rows), 1)).astype(jnp.bfloat16)
    rank = jnp.sum(cells * dot(cells.astype(jnp.bfloat16), earlier), axis=0, keepdims=True)
    counts = jnp.minimum(jnp.sum(cells, axis=1, keepdims=True), float(CELL))
    over = rank >= float(CELL)
    over_team = in_team * over.astype(jnp.float32)
    order = jnp.sum(
        over_team * dot(over_team.astype(jnp.bfloat16), earlier), axis=0, keepdims=True
    )
    filled = [
        jnp.sum(in_team * counts[16 * c : 16 * c + 16], axis=0, keepdims=True) for c in range(4)
    ]
    free0 = CELL - filled[0]
    free1 = free0 + CELL - filled[1]
    free2 = free1 + CELL - filled[2]
    chip = (
        (order >= free0).astype(jnp.int32)
        + (order >= free1).astype(jnp.int32)
        + (order >= free2).astype(jnp.int32)
    )
    spot = jnp.where(
        chip == 0,
        filled[0] + order,
        jnp.where(
            chip == 1,
            filled[1] + order - free0,
            jnp.where(chip == 2, filled[2] + order - free1, filled[3] + order - free2),
        ),
    )
    chip = jnp.where(over, chip, cluster)
    spot = jnp.where(over, spot, rank).astype(jnp.int32)
    cell = team * 4 + chip
    dy = lax.rem(lax.shift_right_logical(team, 2) + (SIDE - place.y), SIDE)
    dz = lax.rem(lax.rem(team, SIDE) + (SIDE - place.z), SIDE)
    dx = lax.rem(chip + (SIDE - place.x), SIDE)
    slot = lax.rem(dy + dz + dx, SIDE) * QUARTER + (dy * SIDE + dz) * CELL + spot
    lane = spot + (place.source % 8) * CELL

    pl.semaphore_wait(barrier, 10)
    for d in range(1, SIDE):
        device = place.at(0, d, 0)[2]
        pl.semaphore_signal(s.line_sem, inc=1, device_id=device, device_id_type=MESH)

    load[2].wait()
    values = s.embed[...].astype(jnp.float32)
    norm = jnp.sum(values * values, axis=1, keepdims=True)
    s.unit[...] = (values * lax.rsqrt(norm + 1e-06)).astype(jnp.bfloat16)

    pl.semaphore_wait(s.line_sem, 3)
    for d in range(1, SIDE):
        device = place.at(0, 0, d)[2]
        pl.semaphore_signal(s.plane_sem, inc=1, device_id=device, device_id_type=MESH)

    in_cell = (iota((CELLS, rows), 0) == cell).astype(jnp.float32)
    at_lane = (iota((LANES, rows), 0) == lane).astype(jnp.bfloat16)
    labels = (in_cell * (cluster + 1).astype(jnp.float32)).astype(jnp.bfloat16)
    s.meta[...] = dot_t(labels, at_lane).reshape(CELLS, 1, LANES)

    send, left = s.send, s.left

    def landing(index):
        return pl.ds(pl.multiple_of(index * CELL, CELL), CELL)

    for phase in range(SIDE):
        base = phase * QUARTER
        chosen = (iota((QUARTER, rows), 0) + base == slot).astype(jnp.bfloat16)
        send[base : base + QUARTER] = dot(chosen, s.unit[...]).astype(jnp.bfloat16)
        if phase == 0:
            pl.semaphore_wait(s.plane_sem, 3)
            pltpu.make_async_copy(
                send.at[pl.ds(0, CELL)], left.at[landing(place.source)], s.recv_sems.at[0]
            ).start()
            pltpu.make_async_copy(
                s.meta.at[pl.ds(place.cell, 1)],
                s.meta_in.at[pl.ds(place.source, 1)],
                s.meta_sem,
            ).start()

        def send_cell(index, carry, phase=phase, base=base):
            target, _, device = place.offset(phase, index)
            pltpu.make_async_remote_copy(
                src_ref=send.at[landing(phase * 16 + index)],
                dst_ref=left.at[landing(place.source)],
                send_sem=s.send_sems.at[0],
                recv_sem=s.recv_sems.at[phase],
                device_id=device,
                device_id_type=MESH,
            ).start()
            pltpu.make_async_remote_copy(
                src_ref=s.meta.at[pl.ds(target, 1)],
                dst_ref=s.meta_in.at[pl.ds(place.source, 1)],
                send_sem=s.send_sems.at[1],
                recv_sem=s.meta_sem,
                device_id=device,
                device_id_type=MESH,
            ).start()
            return carry

        lax.fori_loop(1 if phase == 0 else 0, 16, send_cell, 0)
    return in_cell, at_lane, team, cluster, chip


def arrived(place, phase):
    base = ((place.sum + SIDE - phase) % SIDE) * QUARTER
    return pl.ds(pl.multiple_of(base, QUARTER), QUARTER)


def to_sources(place, source_ref, dest_ref, send_sem, recv_sem):
    def send_one(index, carry):
        _, source, device = place.offset(index // 16, index % 16)
        pltpu.make_async_remote_copy(
            src_ref=source_ref.at[pl.ds(source // 8, 1)],
            dst_ref=dest_ref.at[pl.ds(place.cell, 1)],
            send_sem=send_sem,
            recv_sem=recv_sem,
            device_id=device,
            device_id_type=MESH,
        ).start()
        return carry

    lax.fori_loop(1, CELLS, send_one, 0)
    pltpu.make_async_copy(
        source_ref.at[pl.ds(place.source // 8, 1)], dest_ref.at[pl.ds(place.cell, 1)], recv_sem
    ).start()


def wait_sent(s):
    sent = pl.ds(0, SLOTS - CELL)
    wait_for(s.send.at[sent], s.send_sems.at[0])
    sent = pl.ds(0, CELLS - 1)
    wait_for(s.meta.at[sent], s.send_sems.at[1])


def team_kernel(names, *refs):
    s = types.SimpleNamespace(**dict(zip(names, refs)))
    place = Place()
    in_cell, at_lane, team, cluster, chip = regroup(place, s)
    left, other = s.left, s.other
    left[SLOTS + FORWARD :] = jnp.zeros((LEFT_SPILL - FORWARD, left.shape[1]), jnp.bfloat16)

    def to_pair(src, dst, index):
        copy = pltpu.make_async_remote_copy(
            src_ref=src,
            dst_ref=dst,
            send_sem=s.pair_sems.at[0, index],
            recv_sem=s.pair_sems.at[1, index],
            device_id=place.sibling,
            device_id_type=MESH,
        )
        copy.start()
        return copy

    shared = []
    for phase in range(SIDE):
        part = arrived(place, phase)
        wait_for(left.at[part], s.recv_sems.at[phase])
        shared.append(to_pair(left.at[part], other.at[part], phase))
    wait_for(s.meta_in, s.meta_sem)

    label = jnp.sum(s.meta_in[...].reshape(8, 8, LANES), axis=1)
    own = (place.x + 1).astype(jnp.float32)
    below = (iota((LANES, LANES), 0) < iota((LANES, LANES), 1)).astype(jnp.bfloat16)
    hits = [
        (label == (lax.rem(place.x + d, SIDE) + 1).astype(jnp.float32)).astype(jnp.float32)
        for d in range(1, SIDE)
    ]
    hit = jnp.concatenate(hits, axis=0)
    within = dot(hit.astype(jnp.bfloat16), below)
    totals = jnp.sum(hit, axis=1, keepdims=True)
    places = jnp.full((8, LANES), -1.0, jnp.float32)
    worst = jnp.zeros((1, 1), jnp.float32)
    row, col = iota((8, 8), 0), iota((8, 8), 1)
    for d in range(3):
        total = totals[8 * d : 8 * d + 8]
        spread = jnp.broadcast_to(total, (8, 8))
        before = jnp.sum(jnp.where(row < col, spread, 0.0), axis=0, keepdims=True)
        spread = jnp.broadcast_to(before, (8, 8))
        before = jnp.sum(jnp.where(row == col, spread, 0.0), axis=1, keepdims=True)
        position = within[8 * d : 8 * d + 8] + before
        places = jnp.where(
            (hits[d] > 0.0) & (position < float(SPILL)), position + float(SPILL * d), places
        )
        worst = jnp.maximum(worst, jnp.sum(total, axis=0, keepdims=True))
    failed = jnp.broadcast_to((worst > float(SPILL)).astype(jnp.float32), (8, LANES))
    select, forward = s.select, s.forward
    for q in range(8):
        select[:, q * LANES : (q + 1) * LANES] = (
            iota((FORWARD, LANES), 0).astype(jnp.float32) == places[q : q + 1]
        ).astype(jnp.bfloat16)
    chosen = select[...]
    taken = jnp.sum(chosen.astype(jnp.float32), axis=1, keepdims=True)
    moved = dot(chosen, left[0:SLOTS])
    mark = jnp.where((iota((FORWARD, LANES), 1) == 0) & (taken < 0.5), EMPTY, 0.0)
    forward[:, 0:LANES] = (moved[:, 0:LANES] + mark).astype(jnp.bfloat16)
    forward[:, LANES:] = moved[:, LANES:].astype(jnp.bfloat16)
    to_line = []
    for d in range(3):
        copy = pltpu.make_async_remote_copy(
            src_ref=forward.at[pl.ds(d * SPILL, SPILL)],
            dst_ref=left.at[pl.ds(SLOTS + d * SPILL, SPILL)],
            send_sem=s.spill_sems.at[0, d],
            recv_sem=s.spill_sems.at[1, d],
            device_id=place.at(0, 0, d + 1)[2],
            device_id_type=MESH,
        )
        copy.start()
        to_line.append(copy)
    s.label_out[0:8] = label
    s.label_out[8:16] = failed
    copy_label = to_pair(s.label_out, s.label_in, 4)
    s.places_out[...] = places.reshape(8, 1, LANES)
    to_sources(place, s.places_out, s.places_in, s.send_sems.at[2], s.places_sem)

    def set_bias(ref, tags):
        for q in range(8):
            ref[q * LANES : (q + 1) * LANES, 0:1] = jnp.where(column(tags, q) == own, 0.0, NONE)

    def against(right, right_bias, first, count, same):
        def one(index, best):
            base = pl.multiple_of(index * QUARTER, QUARTER)
            part = pl.ds(base, QUARTER)
            scores = dot_t(right[part], left[first : first + count]) + right_bias[part, 0:1]
            if same:
                scores = jnp.where(
                    iota((QUARTER, count), 0) + base == iota((QUARTER, count), 1), NONE, scores
                )
            return jnp.maximum(best, fold(scores))

        start = jnp.full((8, count), NONE, jnp.float32)
        return lax.fori_loop(0, SLOTS // QUARTER, one, start)

    bias, other_bias = s.bias, s.other_bias
    set_bias(bias, label)
    best_main = against(left, bias, 0, SLOTS, True)
    copy_label.wait()
    set_bias(other_bias, s.label_in[0:8])
    for copy in shared:
        copy.wait()
    best_main = jnp.maximum(best_main, against(other, other_bias, 0, SLOTS, False))

    for copy in to_line:
        copy.wait()
    spill_pair = to_pair(left.at[pl.ds(SLOTS, FORWARD)], s.other_spill, 5)
    best_spill = against(left, bias, SLOTS, LEFT_SPILL, False)
    best_spill = jnp.maximum(best_spill, against(other, other_bias, SLOTS, LEFT_SPILL, False))

    def against_spill(right, same):
        scores = dot_t(right, left[...]) + jnp.where(
            right[:, 0:1].astype(jnp.float32) > 1.5, NONE, 0.0
        )
        if same:
            scores = jnp.where(
                iota(scores.shape, 0) + SLOTS == iota(scores.shape, 1), NONE, scores
            )
        return fold(scores)

    best_all = against_spill(left[SLOTS : SLOTS + FORWARD], True)
    rows = cluster.shape[1]
    wait_for(s.places_in, s.places_sem)
    held = dot(s.places_in[...].reshape(CELLS, LANES).astype(jnp.bfloat16), at_lane)
    held = jnp.sum(held * in_cell, axis=0, keepdims=True).astype(jnp.int32)
    at_held = (iota((LEFT_SPILL, rows), 0) == held).astype(jnp.bfloat16)
    in_own = (iota((CELLS, rows), 0) == team * 4 + cluster).astype(jnp.float32)
    spill_pair.wait()
    best_all = jnp.maximum(best_all, against_spill(s.other_spill[...], False))
    best_main = jnp.max(jnp.maximum(best_main, best_all[:, 0:SLOTS]), axis=0, keepdims=True)
    best_spill = jnp.max(jnp.maximum(best_spill, best_all[:, SLOTS:]), axis=0, keepdims=True)

    failed = jnp.maximum(failed, s.label_in[8:16])[0:1]
    best_out = s.best_out
    for q in range(8):
        part = best_main[:, q * LANES : (q + 1) * LANES]
        best_out[q, :, 0:LANES] = jnp.where(failed > 0.0, FAILED, part)
        best_out[q, :, LANES:] = best_spill
    to_sources(place, best_out, s.best_in, s.send_sems.at[3], s.best_sem)
    wait_for(s.best_in, s.best_sem)
    found = s.best_in[...].reshape(CELLS, LANES + LEFT_SPILL)
    worst = jnp.max(jnp.max(found, axis=1, keepdims=True), axis=0, keepdims=True)
    straight = sum(dot(piece, at_lane) for piece in split3(found[:, 0:LANES]))
    straight = jnp.sum(straight * in_cell, axis=0, keepdims=True)
    moved = sum(dot(piece, at_held) for piece in split3(found[:, LANES:]))
    moved = jnp.sum(moved * in_own, axis=0, keepdims=True)
    score = jnp.maximum(jnp.where(chip == cluster, straight, moved), -1.0)
    s.out[...] = jnp.where(worst > 4.0, FAILED, score)

    wait_sent(s)
    sent = pl.ds(0, CELLS - 1)
    wait_for(s.places_in.at[sent], s.send_sems.at[2])
    wait_for(s.best_in.at[sent], s.send_sems.at[3])


def general_kernel(names, *refs):
    s = types.SimpleNamespace(**dict(zip(names, refs)))
    place = Place()
    in_cell, at_lane, _, _, _ = regroup(place, s)
    left = s.left
    for phase in range(SIDE):
        wait_for(left.at[arrived(place, phase)], s.recv_sems.at[phase])
    wait_for(s.meta_in, s.meta_sem)
    label = jnp.sum(s.meta_in[...].reshape(8, 8, LANES), axis=1)
    s.label_out[...] = label
    copies = []
    for block in range(1, 8):
        for index, (src, dst) in enumerate(((left, s.gather), (s.label_out, s.tags))):
            copy = pltpu.make_async_remote_copy(
                src_ref=src,
                dst_ref=dst.at[block - 1],
                send_sem=s.line_sems.at[0, index, block - 1],
                recv_sem=s.line_sems.at[1, index, block - 1],
                device_id=place.at(0, 0, block // 2, block % 2)[2],
                device_id_type=MESH,
            )
            copy.start()
            copies.append(copy)
    left_label = jnp.concatenate([label[q : q + 1] for q in range(8)], axis=1)

    def against(right, tags, same):
        for q in range(8):
            s.bias[q * LANES : (q + 1) * LANES, 0:1] = column(tags, q)

        def one(index, best):
            base = pl.multiple_of(index * QUARTER, QUARTER)
            part = pl.ds(base, QUARTER)
            scores = dot_t(right[part], left[...])
            counts = s.bias[part, 0:1] == left_label
            if same:
                shape = (QUARTER, SLOTS)
                counts = counts & (iota(shape, 0) + base != iota(shape, 1))
            return jnp.maximum(best, fold(jnp.where(counts, scores, NONE)))

        start = jnp.full((8, SLOTS), NONE, jnp.float32)
        return lax.fori_loop(0, SLOTS // QUARTER, one, start)

    best = against(left, label, True)
    for copy in copies:
        copy.wait()

    def block(index, best):
        return jnp.maximum(best, against(s.gather.at[index], s.tags[index], False))

    best = jnp.max(lax.fori_loop(0, 7, block, best), axis=0, keepdims=True)
    for q in range(8):
        s.best_out[q] = best[:, q * LANES : (q + 1) * LANES]
    to_sources(place, s.best_out, s.best_in, s.send_sems.at[2], s.best_sem)
    wait_for(s.best_in, s.best_sem)
    found = s.best_in[...].reshape(CELLS, LANES)
    score = sum(dot(piece, at_lane) for piece in split3(found))
    s.out[...] = jnp.maximum(jnp.sum(score * in_cell, axis=0, keepdims=True), -1.0)
    wait_sent(s)
    wait_for(s.best_in.at[pl.ds(0, CELLS - 1)], s.send_sems.at[2])


def call(kernel, name, collective, extra, embed, destination, cluster):
    rows, features = embed.shape
    bf16, f32, i32 = jnp.bfloat16, jnp.float32, jnp.int32
    vmem, dma = pltpu.VMEM, pltpu.SemaphoreType.DMA
    scratch = dict(
        dest=vmem((1, rows), i32),
        cluster=vmem((1, rows), i32),
        embed=vmem((rows, features), bf16),
        unit=vmem((rows, features), bf16),
        send=vmem((SLOTS, features), bf16),
        meta=vmem((CELLS, 1, LANES), f32),
        meta_in=vmem((CELLS, 1, LANES), f32),
        bias=vmem((SLOTS, LANES), f32),
        line_sem=pltpu.SemaphoreType.REGULAR,
        plane_sem=pltpu.SemaphoreType.REGULAR,
        load_sems=dma((3,)),
        send_sems=dma((4,)),
        recv_sems=dma((SIDE,)),
        meta_sem=dma,
        best_sem=dma,
        **extra(features),
    )
    names = ("dest_hbm", "cluster_hbm", "embed_hbm", "out", *scratch)
    return pl.pallas_call(
        functools.partial(kernel, names),
        out_shape=jax.ShapeDtypeStruct((1, rows), f32),
        in_specs=[pl.BlockSpec(memory_space=pl.ANY)] * 3,
        out_specs=pl.BlockSpec(memory_space=pltpu.VMEM),
        scratch_shapes=list(scratch.values()),
        compiler_params=pltpu.CompilerParams(
            collective_id=collective, has_side_effects=True, vmem_limit_bytes=40 * 2**20
        ),
        name=name,
    )(destination.reshape(1, rows), cluster.reshape(1, rows), embed)


def team_scratch(features):
    bf16, f32, vmem, dma = jnp.bfloat16, jnp.float32, pltpu.VMEM, pltpu.SemaphoreType.DMA
    return dict(
        left=vmem((SLOTS + LEFT_SPILL, features), bf16),
        other=vmem((SLOTS, features), bf16),
        other_spill=vmem((FORWARD, features), bf16),
        select=vmem((FORWARD, SLOTS), bf16),
        forward=vmem((FORWARD, features), bf16),
        label_out=vmem((16, LANES), f32),
        label_in=vmem((16, LANES), f32),
        other_bias=vmem((SLOTS, LANES), f32),
        places_out=vmem((8, 1, LANES), f32),
        places_in=vmem((CELLS, 1, LANES), f32),
        best_out=vmem((8, 1, LANES + LEFT_SPILL), f32),
        best_in=vmem((CELLS, 1, LANES + LEFT_SPILL), f32),
        places_sem=dma,
        pair_sems=dma((2, 6)),
        spill_sems=dma((2, 3)),
    )


def general_scratch(features):
    bf16, f32, vmem, dma = jnp.bfloat16, jnp.float32, pltpu.VMEM, pltpu.SemaphoreType.DMA
    return dict(
        left=vmem((SLOTS, features), bf16),
        gather=vmem((7, SLOTS, features), bf16),
        label_out=vmem((8, LANES), f32),
        tags=vmem((7, 8, LANES), f32),
        best_out=vmem((8, 1, LANES), f32),
        best_in=vmem((CELLS, 1, LANES), f32),
        line_sems=dma((2, 2, 7)),
    )


def shards(embed, destination, cluster):
    rows = embed.shape[0]
    scores = call(team_kernel, "team_scores", 0, team_scratch, embed, destination, cluster)

    def general(*args):
        return call(general_kernel, "general_scores", 1, general_scratch, *args).reshape(rows)

    return lax.cond(
        scores[0, 0] > 4.0,
        general,
        lambda *unused: scores.reshape(rows),
        embed,
        destination,
        cluster,
    )


def solution(mesh):
    in_specs = (P(("group", "member"), None), P(("group", "member")), P(("group", "member")))
    out_specs = P(("group", "member"))
    return jax.shard_map(shards, mesh=mesh, in_specs=in_specs, out_specs=out_specs, check_vma=False)
```

```python
import functools
import types

import jax
import jax.numpy as jnp
from jax import lax
from jax.experimental import pallas as pl
from jax.experimental.pallas import tpu as pltpu
from jax.sharding import PartitionSpec as P

MESH = pl.DeviceIdType.MESH
SIDE = 4
CELLS = 64
CELL = 16
SPILL = 80
LANES = 128
QUARTER = 256
SLOTS = CELLS * CELL
FORWARD = 3 * SPILL
LEFT_SPILL = 256
NONE = -4.0
META_AFTER = 0
ENTRY = 3
FAILED = 8.0
EMPTY = 2.0


def split3(value):
    high = value.astype(jnp.bfloat16)
    rest = value - high.astype(jnp.float32)
    mid = rest.astype(jnp.bfloat16)
    low = (rest - mid.astype(jnp.float32)).astype(jnp.bfloat16)
    return high, mid, low


def iota(shape, dim):
    return lax.broadcasted_iota(jnp.int32, shape, dim)


def dot(left, right):
    return jnp.dot(left, right, preferred_element_type=jnp.float32)


def dot_t(left, right):
    return lax.dot_general(left, right, (((1,), (1,)), ((), ())), preferred_element_type=jnp.float32)


def fold(scores):
    rows, columns = scores.shape
    return jnp.max(scores.reshape(rows // 8, 8, columns), axis=0)


def column(tags, index):
    return jnp.transpose(tags)[:, index : index + 1]


class Place:
    def __init__(self):
        group = lax.axis_index("group")
        member = lax.axis_index("member")
        y, z = group // SIDE, group % SIDE
        x, self.core = member // 2, member % 2
        self.ys = [y] + [(y + d) % SIDE for d in range(1, SIDE)]
        self.zs = [z] + [(z + d) % SIDE for d in range(1, SIDE)]
        self.xs = [x] + [(x + d) % SIDE for d in range(1, SIDE)]
        self.y, self.z, self.x = y, z, x
        self.cell = group * SIDE + x
        self.sum = (y + z + x) % SIDE
        self.sums = [self.sum] + [(self.sum + d) % SIDE for d in range(1, SIDE)]
        self.source = self.sum * 16 + group
        self.halves = [value // 2 for value in self.ys]
        self.sibling = {"group": group, "member": x * 2 + 1 - self.core}

    def at(self, dy, dz, dx):
        return {"group": self.ys[dy] * SIDE + self.zs[dz], "member": self.xs[dx] * 2 + self.core}

    def cell_at(self, dy, dz, dx):
        return (self.ys[dy] * SIDE + self.zs[dz]) * SIDE + self.xs[dx]

    def eight_at(self, dy, dz, dx):
        return self.sums[(dy + dz + dx) % SIDE] * 2 + self.halves[dy]


def offsets(phase):
    return [(dy, dz, (phase - dy - dz) % SIDE) for dy in range(SIDE) for dz in range(SIDE)]


OTHERS = [offset for phase in range(SIDE) for offset in offsets(phase)][1:]


def wait_for(ref, sem):
    pltpu.make_async_copy(ref, ref, sem).wait()


def greet(place, s):
    barrier = pltpu.get_barrier_semaphore()
    for d in range(1, SIDE):
        for offset in ((d, 0, 0), (0, d, 0), (0, 0, d)):
            device = place.at(*offset)
            pl.semaphore_signal(barrier, inc=1, device_id=device, device_id_type=MESH)
    pl.semaphore_signal(barrier, inc=1, device_id=place.sibling, device_id_type=MESH)
    return barrier


def regroup(place, s):
    load = [
        pltpu.make_async_copy(src, dst, s.load_sems.at[n])
        for n, (src, dst) in enumerate(
            ((s.dest_hbm, s.dest), (s.cluster_hbm, s.cluster), (s.embed_hbm, s.embed))
        )
    ]
    for copy in load:
        copy.start()
    barrier = greet(place, s)
    load[0].wait()
    load[1].wait()

    rows = s.dest.shape[1]
    team = lax.shift_right_logical(s.dest[...], 3)
    cluster = s.cluster[...]
    in_team = (iota((16, rows), 0) == team).astype(jnp.float32)
    cells = jnp.concatenate(
        [in_team * (cluster == c).astype(jnp.float32) for c in range(4)], axis=0
    )
    earlier = (iota((rows, rows), 0) < iota((rows, rows), 1)).astype(jnp.bfloat16)
    rank = jnp.sum(cells * dot(cells.astype(jnp.bfloat16), earlier), axis=0, keepdims=True)
    counts = jnp.minimum(jnp.sum(cells, axis=1, keepdims=True), float(CELL))
    over = rank >= float(CELL)
    over_team = in_team * over.astype(jnp.float32)
    order = jnp.sum(
        over_team * dot(over_team.astype(jnp.bfloat16), earlier), axis=0, keepdims=True
    )
    filled = [
        jnp.sum(in_team * counts[16 * c : 16 * c + 16], axis=0, keepdims=True) for c in range(4)
    ]
    free0 = CELL - filled[0]
    free1 = free0 + CELL - filled[1]
    free2 = free1 + CELL - filled[2]
    chip = (
        (order >= free0).astype(jnp.int32)
        + (order >= free1).astype(jnp.int32)
        + (order >= free2).astype(jnp.int32)
    )
    spot = jnp.where(
        chip == 0,
        filled[0] + order,
        jnp.where(
            chip == 1,
            filled[1] + order - free0,
            jnp.where(chip == 2, filled[2] + order - free1, filled[3] + order - free2),
        ),
    )
    chip = jnp.where(over, chip, cluster)
    spot = jnp.where(over, spot, rank).astype(jnp.int32)
    cell = team * 4 + chip
    dy = lax.rem(lax.shift_right_logical(team, 2) + (SIDE - place.y), SIDE)
    dz = lax.rem(lax.rem(team, SIDE) + (SIDE - place.z), SIDE)
    dx = lax.rem(chip + (SIDE - place.x), SIDE)
    slot = lax.rem(dy + dz + dx, SIDE) * QUARTER + (dy * SIDE + dz) * CELL + spot
    lane = spot + (place.source % 8) * CELL

    pl.semaphore_wait(barrier, 10)
    for d in range(1, SIDE):
        device = place.at(0, d, 0)
        pl.semaphore_signal(s.line_sem, inc=1, device_id=device, device_id_type=MESH)

    load[2].wait()
    values = s.embed[...].astype(jnp.float32)
    norm = jnp.sum(values * values, axis=1, keepdims=True)
    s.unit[...] = (values * lax.rsqrt(norm + 1e-06)).astype(jnp.bfloat16)

    pl.semaphore_wait(s.line_sem, 3)
    for d in range(1, SIDE):
        device = place.at(0, 0, d)
        pl.semaphore_signal(s.plane_sem, inc=1, device_id=device, device_id_type=MESH)

    in_cell = (iota((CELLS, rows), 0) == cell).astype(jnp.float32)
    at_lane = (iota((LANES, rows), 0) == lane).astype(jnp.bfloat16)
    labels = (in_cell * (cluster + 1).astype(jnp.float32)).astype(jnp.bfloat16)
    s.meta[...] = dot_t(labels, at_lane).reshape(CELLS, 1, LANES)

    send, left = s.send, s.left

    def landing(index):
        return pl.ds(pl.multiple_of(index * CELL, CELL), CELL)

    for phase in range(SIDE):
        base = phase * QUARTER
        chosen = (iota((QUARTER, rows), 0) + base == slot).astype(jnp.bfloat16)
        send[base : base + QUARTER] = dot(chosen, s.unit[...]).astype(jnp.bfloat16)
        if phase == 0:
            pl.semaphore_wait(s.plane_sem, 3)
            pltpu.make_async_copy(
                send.at[pl.ds(0, CELL)], left.at[landing(place.source)], s.recv_sems.at[0]
            ).start()

        for index, offset in enumerate(offsets(phase)):
            if any(offset):
                pltpu.make_async_remote_copy(
                    src_ref=send.at[landing(phase * 16 + index)],
                    dst_ref=left.at[landing(place.source)],
                    send_sem=s.send_sems.at[0],
                    recv_sem=s.recv_sems.at[phase],
                    device_id=place.at(*offset),
                    device_id_type=MESH,
                ).start()
        if phase == META_AFTER:
            send_labels(place, s)
    return in_cell, at_lane, team, cluster, chip, lane


def send_labels(place, s):
    for offset in OTHERS:
        pltpu.make_async_remote_copy(
            src_ref=s.meta.at[pl.ds(place.cell_at(*offset), 1)],
            dst_ref=s.meta_in.at[pl.ds(place.source, 1)],
            send_sem=s.send_sems.at[1],
            recv_sem=s.meta_sem,
            device_id=place.at(*offset),
            device_id_type=MESH,
        ).start()
    pltpu.make_async_copy(
        s.meta.at[pl.ds(place.cell, 1)], s.meta_in.at[pl.ds(place.source, 1)], s.meta_sem
    ).start()


def quarter(place, phase):
    if isinstance(phase, int):
        return place.sums[-phase % SIDE]
    return (place.sum + SIDE - phase) % SIDE


def rows_of(index):
    return pl.ds(pl.multiple_of(index * QUARTER, QUARTER), QUARTER)


def arrived(place, phase):
    return rows_of(quarter(place, phase))


def to_sources(place, source_ref, dest_ref, size, send_sem, recv_sem):
    for offset in OTHERS:
        pltpu.make_async_remote_copy(
            src_ref=source_ref.at[pl.ds(place.eight_at(*offset) * size, size)],
            dst_ref=dest_ref.at[pl.ds(place.cell * size, size)],
            send_sem=send_sem,
            recv_sem=recv_sem,
            device_id=place.at(*offset),
            device_id_type=MESH,
        ).start()
    pltpu.make_async_copy(
        source_ref.at[pl.ds(place.source // 8 * size, size)],
        dest_ref.at[pl.ds(place.cell * size, size)],
        recv_sem,
    ).start()


def wait_sent(s):
    sent = pl.ds(0, SLOTS - CELL)
    wait_for(s.send.at[sent], s.send_sems.at[0])
    sent = pl.ds(0, CELLS - 1)
    wait_for(s.meta.at[sent], s.send_sems.at[1])


def team_kernel(names, *refs):
    s = types.SimpleNamespace(**dict(zip(names, refs)))
    place = Place()
    in_cell, at_lane, team, cluster, chip, lane = regroup(place, s)
    left, other = s.left, s.other
    left[SLOTS + FORWARD :] = jnp.zeros((LEFT_SPILL - FORWARD, left.shape[1]), jnp.bfloat16)

    def to_pair(src, dst, index):
        copy = pltpu.make_async_remote_copy(
            src_ref=src,
            dst_ref=dst,
            send_sem=s.pair_sems.at[0, index],
            recv_sem=s.pair_sems.at[1, index],
            device_id=place.sibling,
            device_id_type=MESH,
        )
        copy.start()
        return copy

    wait_for(s.meta_in, s.meta_sem)
    label = jnp.sum(s.meta_in[...].reshape(8, 8, LANES), axis=1)
    own = (place.x + 1).astype(jnp.float32)
    below = (iota((LANES, LANES), 0) < iota((LANES, LANES), 1)).astype(jnp.bfloat16)
    hits = [
        (label == (lax.rem(place.x + d, SIDE) + 1).astype(jnp.float32)).astype(jnp.float32)
        for d in range(1, SIDE)
    ]
    hit = jnp.concatenate(hits, axis=0)
    within = dot(hit.astype(jnp.bfloat16), below)
    totals = jnp.sum(hit, axis=1, keepdims=True)
    places = jnp.full((8, LANES), -1.0, jnp.float32)
    worst = jnp.zeros((1, 1), jnp.float32)
    row, col = iota((8, 8), 0), iota((8, 8), 1)
    for d in range(3):
        total = totals[8 * d : 8 * d + 8]
        spread = jnp.broadcast_to(total, (8, 8))
        before = jnp.sum(jnp.where(row < col, spread, 0.0), axis=0, keepdims=True)
        spread = jnp.broadcast_to(before, (8, 8))
        before = jnp.sum(jnp.where(row == col, spread, 0.0), axis=1, keepdims=True)
        position = within[8 * d : 8 * d + 8] + before
        places = jnp.where(
            (hits[d] > 0.0) & (position < float(SPILL)), position + float(SPILL * d), places
        )
        worst = jnp.maximum(worst, jnp.sum(total, axis=0, keepdims=True))
    failed = jnp.broadcast_to((worst > float(SPILL)).astype(jnp.float32), (8, LANES))
    s.label_out[0:8] = label
    s.label_out[8:16] = failed
    copy_label = to_pair(s.label_out, s.label_in, 4)
    s.places_out[...] = places.reshape(8, 1, LANES)
    to_sources(place, s.places_out, s.places_in, 1, s.send_sems.at[2], s.places_sem)
    select, forward = s.select, s.forward
    for q in range(8):
        select[q // 2, :, (q % 2) * LANES : (q % 2 + 1) * LANES] = (
            iota((FORWARD, LANES), 0).astype(jnp.float32) == places[q : q + 1]
        ).astype(jnp.bfloat16)
    taken = jnp.zeros((FORWARD, 1), jnp.float32)
    for q in range(SIDE):
        taken = taken + jnp.sum(select[q].astype(jnp.float32), axis=1, keepdims=True)
    mark = jnp.where((iota((FORWARD, LANES), 1) == 0) & (taken < 0.5), EMPTY, 0.0)
    s.moved[...] = jnp.zeros(s.moved.shape, jnp.float32)
    s.moved[:, 0:LANES] = mark
    s.best[...] = jnp.full(s.best.shape, NONE, jnp.float32)

    def set_bias(ref, tags):
        for q in range(8):
            ref[q * LANES : (q + 1) * LANES, 0:1] = jnp.where(column(tags, q) == own, 0.0, NONE)

    bias, other_bias = s.bias, s.other_bias
    set_bias(bias, label)
    copy_label.wait()
    set_bias(other_bias, s.label_in[0:8])

    def block(right, right_bias, index, target, same=False):
        part = rows_of(index)
        scores = dot_t(right[part], left[rows_of(target)]) + right_bias[part, 0:1]
        if same:
            shape = (QUARTER, QUARTER)
            scores = jnp.where(iota(shape, 0) == iota(shape, 1), NONE, scores)
        s.best[target] = jnp.maximum(s.best[target], fold(scores))

    def blocks(right, right_bias, phase, same):
        last = quarter(place, phase)
        block(right, right_bias, last, last, same)

        def one(index, carry):
            first = quarter(place, index)
            block(right, right_bias, last, first)
            block(right, right_bias, first, last)
            return carry

        lax.fori_loop(0, phase, one, 0)

    shared = []
    for phase in range(SIDE):
        part = arrived(place, phase)
        wait_for(left.at[part], s.recv_sems.at[phase])
        shared.append(to_pair(left.at[part], other.at[part], phase))
        s.moved[...] += dot(select[quarter(place, phase)], left[part])
        if phase < SIDE - 1:
            blocks(left, bias, phase, True)
            if phase > 0:
                shared[phase - 1].wait()
                blocks(other, other_bias, phase - 1, False)

    forward[...] = s.moved[...].astype(jnp.bfloat16)
    to_line = []
    for d in (1, 0, 2):
        copy = pltpu.make_async_remote_copy(
            src_ref=forward.at[pl.ds(d * SPILL, SPILL)],
            dst_ref=left.at[pl.ds(SLOTS + d * SPILL, SPILL)],
            send_sem=s.spill_sems.at[0, d],
            recv_sem=s.spill_sems.at[1, d],
            device_id=place.at(0, 0, d + 1),
            device_id_type=MESH,
        )
        copy.start()
        to_line.append(copy)
    blocks(left, bias, SIDE - 1, True)
    for phase in (SIDE - 2, SIDE - 1):
        shared[phase].wait()
        blocks(other, other_bias, phase, False)

    rows = cluster.shape[1]
    wait_for(s.places_in, s.places_sem)
    held = dot(s.places_in[...].reshape(CELLS, LANES).astype(jnp.bfloat16), at_lane)
    held = jnp.sum(held * in_cell, axis=0, keepdims=True).astype(jnp.int32)
    straight = chip == cluster
    entry = ENTRY * (team * 4 + cluster) + jnp.where(
        straight, 0, 1 + (held >= LANES).astype(jnp.int32)
    )
    in_entry = (iota((ENTRY * CELLS, rows), 0) == entry).astype(jnp.float32)
    spot = jnp.where(straight, lane, jnp.where(held >= LANES, held - LANES, held))
    at_spot = (iota((LANES, rows), 0) == spot).astype(jnp.bfloat16)

    for copy in to_line:
        copy.wait()
    spill_pair = to_pair(left.at[pl.ds(SLOTS, FORWARD)], s.other_spill, 5)

    def against(right, right_bias, best):
        def one(index, best):
            part = rows_of(index)
            scores = dot_t(right[part], left[SLOTS:]) + right_bias[part, 0:1]
            return jnp.maximum(best, fold(scores))

        return lax.fori_loop(0, SIDE, one, best)

    def against_spill(right, same):
        scores = dot_t(right, left[...]) + jnp.where(
            right[:, 0:1].astype(jnp.float32) > 1.5, NONE, 0.0
        )
        if same:
            scores = jnp.where(
                iota(scores.shape, 0) + SLOTS == iota(scores.shape, 1), NONE, scores
            )
        return fold(scores)

    best_spill = jnp.full((8, LEFT_SPILL), NONE, jnp.float32)
    best_spill = against(left, bias, best_spill)
    best_spill = against(other, other_bias, best_spill)
    best_all = against_spill(left[SLOTS : SLOTS + FORWARD], True)
    spill_pair.wait()
    best_all = jnp.maximum(best_all, against_spill(s.other_spill[...], False))
    best_spill = jnp.max(jnp.maximum(best_spill, best_all[:, SLOTS:]), axis=0, keepdims=True)

    failed = jnp.maximum(failed, s.label_in[8:16])[0:1]
    best_out = s.best_out
    for q in range(8):
        half = slice((q % 2) * LANES, (q % 2 + 1) * LANES)
        part = jnp.maximum(s.best[q // 2, :, half], best_all[:, q * LANES : (q + 1) * LANES])
        part = jnp.max(part, axis=0, keepdims=True)
        best_out[q * ENTRY] = jnp.where(failed > 0.0, FAILED, part)
        for half in range(LEFT_SPILL // LANES):
            best_out[q * ENTRY + 1 + half] = best_spill[:, half * LANES : (half + 1) * LANES]
    to_sources(place, best_out, s.best_in, ENTRY, s.send_sems.at[3], s.best_sem)
    wait_for(s.best_in, s.best_sem)
    found = s.best_in[...].reshape(ENTRY * CELLS, LANES)
    worst = jnp.max(jnp.max(found, axis=0, keepdims=True), axis=1, keepdims=True)
    picked = sum(dot(piece, at_spot) for piece in split3(found))
    score = jnp.maximum(jnp.sum(picked * in_entry, axis=0, keepdims=True), -1.0)
    s.out[...] = jnp.where(worst > 4.0, FAILED, score)

    wait_sent(s)
    sent = pl.ds(0, CELLS - 1)
    wait_for(s.places_in.at[sent], s.send_sems.at[2])
    wait_for(s.best_in.at[pl.ds(0, ENTRY * (CELLS - 1))], s.send_sems.at[3])


def general_kernel(names, *refs):
    s = types.SimpleNamespace(**dict(zip(names, refs)))
    place = Place()
    in_cell, at_lane, *_ = regroup(place, s)
    left = s.left
    for phase in range(SIDE):
        wait_for(left.at[arrived(place, phase)], s.recv_sems.at[phase])
    wait_for(s.meta_in, s.meta_sem)
    label = jnp.sum(s.meta_in[...].reshape(8, 8, LANES), axis=1)
    s.label_out[...] = label
    copies = []
    for block in range(1, 8):
        for index, (src, dst) in enumerate(((left, s.gather), (s.label_out, s.tags))):
            copy = pltpu.make_async_remote_copy(
                src_ref=src,
                dst_ref=dst.at[block - 1],
                send_sem=s.line_sems.at[0, index, block - 1],
                recv_sem=s.line_sems.at[1, index, block - 1],
                device_id={"member": place.xs[block // 2] * 2 + (place.core + block) % 2},
                device_id_type=MESH,
            )
            copy.start()
            copies.append(copy)
    left_label = jnp.concatenate([label[q : q + 1] for q in range(8)], axis=1)

    def against(right, tags, same):
        for q in range(8):
            s.bias[q * LANES : (q + 1) * LANES, 0:1] = column(tags, q)

        def one(index, best):
            base = pl.multiple_of(index * QUARTER, QUARTER)
            part = pl.ds(base, QUARTER)
            scores = dot_t(right[part], left[...])
            counts = s.bias[part, 0:1] == left_label
            if same:
                shape = (QUARTER, SLOTS)
                counts = counts & (iota(shape, 0) + base != iota(shape, 1))
            return jnp.maximum(best, fold(jnp.where(counts, scores, NONE)))

        start = jnp.full((8, SLOTS), NONE, jnp.float32)
        return lax.fori_loop(0, SLOTS // QUARTER, one, start)

    best = against(left, label, True)
    for copy in copies:
        copy.wait()

    def block(index, best):
        return jnp.maximum(best, against(s.gather.at[index], s.tags[index], False))

    best = jnp.max(lax.fori_loop(0, 7, block, best), axis=0, keepdims=True)
    for q in range(8):
        s.best_out[q] = best[:, q * LANES : (q + 1) * LANES]
    to_sources(place, s.best_out, s.best_in, 1, s.send_sems.at[2], s.best_sem)
    wait_for(s.best_in, s.best_sem)
    found = s.best_in[...].reshape(CELLS, LANES)
    score = sum(dot(piece, at_lane) for piece in split3(found))
    s.out[...] = jnp.maximum(jnp.sum(score * in_cell, axis=0, keepdims=True), -1.0)
    wait_sent(s)
    wait_for(s.best_in.at[pl.ds(0, CELLS - 1)], s.send_sems.at[2])


def call(kernel, name, collective, extra, embed, destination, cluster):
    rows, features = embed.shape
    bf16, f32, i32 = jnp.bfloat16, jnp.float32, jnp.int32
    vmem, dma = pltpu.VMEM, pltpu.SemaphoreType.DMA
    scratch = dict(
        dest=vmem((1, rows), i32),
        cluster=vmem((1, rows), i32),
        embed=vmem((rows, features), bf16),
        unit=vmem((rows, features), bf16),
        send=vmem((SLOTS, features), bf16),
        meta=vmem((CELLS, 1, LANES), f32),
        meta_in=vmem((CELLS, 1, LANES), f32),
        bias=vmem((SLOTS, LANES), f32),
        line_sem=pltpu.SemaphoreType.REGULAR,
        plane_sem=pltpu.SemaphoreType.REGULAR,
        load_sems=dma((3,)),
        send_sems=dma((4,)),
        recv_sems=dma((SIDE,)),
        meta_sem=dma,
        best_sem=dma,
        **extra(features),
    )
    names = ("dest_hbm", "cluster_hbm", "embed_hbm", "out", *scratch)
    return pl.pallas_call(
        functools.partial(kernel, names),
        out_shape=jax.ShapeDtypeStruct((1, rows), f32),
        in_specs=[pl.BlockSpec(memory_space=pl.ANY)] * 3,
        out_specs=pl.BlockSpec(memory_space=pltpu.VMEM),
        scratch_shapes=list(scratch.values()),
        compiler_params=pltpu.CompilerParams(
            collective_id=collective, has_side_effects=True, vmem_limit_bytes=40 * 2**20
        ),
        name=name,
    )(destination.reshape(1, rows), cluster.reshape(1, rows), embed)


def team_scratch(features):
    bf16, f32, vmem, dma = jnp.bfloat16, jnp.float32, pltpu.VMEM, pltpu.SemaphoreType.DMA
    return dict(
        left=vmem((SLOTS + LEFT_SPILL, features), bf16),
        other=vmem((SLOTS, features), bf16),
        other_spill=vmem((FORWARD, features), bf16),
        select=vmem((SIDE, FORWARD, QUARTER), bf16),
        moved=vmem((FORWARD, features), f32),
        best=vmem((SIDE, 8, QUARTER), f32),
        forward=vmem((FORWARD, features), bf16),
        label_out=vmem((16, LANES), f32),
        label_in=vmem((16, LANES), f32),
        other_bias=vmem((SLOTS, LANES), f32),
        places_out=vmem((8, 1, LANES), f32),
        places_in=vmem((CELLS, 1, LANES), f32),
        best_out=vmem((8 * ENTRY, 1, LANES), f32),
        best_in=vmem((CELLS * ENTRY, 1, LANES), f32),
        places_sem=dma,
        pair_sems=dma((2, 6)),
        spill_sems=dma((2, 3)),
    )


def general_scratch(features):
    bf16, f32, vmem, dma = jnp.bfloat16, jnp.float32, pltpu.VMEM, pltpu.SemaphoreType.DMA
    return dict(
        left=vmem((SLOTS, features), bf16),
        gather=vmem((7, SLOTS, features), bf16),
        label_out=vmem((8, LANES), f32),
        tags=vmem((7, 8, LANES), f32),
        best_out=vmem((8, 1, LANES), f32),
        best_in=vmem((CELLS, 1, LANES), f32),
        line_sems=dma((2, 2, 7)),
    )


def shards(embed, destination, cluster):
    rows = embed.shape[0]
    scores = call(team_kernel, "team_scores", 0, team_scratch, embed, destination, cluster)

    def general(*args):
        return call(general_kernel, "general_scores", 1, general_scratch, *args).reshape(rows)

    return lax.cond(
        scores[0, 0] > 4.0,
        general,
        lambda *unused: scores.reshape(rows),
        embed,
        destination,
        cluster,
    )


def solution(mesh):
    in_specs = (P(("group", "member"), None), P(("group", "member")), P(("group", "member")))
    out_specs = P(("group", "member"))
    return jax.shard_map(shards, mesh=mesh, in_specs=in_specs, out_specs=out_specs, check_vma=False)
```

```python
import functools
import types

import jax
import jax.numpy as jnp
from jax import lax
from jax.experimental import pallas as pl
from jax.experimental.pallas import tpu as pltpu
from jax.sharding import PartitionSpec as P

MESH = pl.DeviceIdType.MESH
SIDE = 4
CELLS = 64
CELL = 16
SPILL = 80
LANES = 128
QUARTER = 256
SLOTS = CELLS * CELL
FORWARD = 3 * SPILL
LEFT_SPILL = 256
NONE = -4.0
META_AFTER = 0
ENTRY = 3
FAILED = 8.0
EMPTY = 2.0
SPILL_ORDER = (1, 0, 2)


def split3(value):
    high = value.astype(jnp.bfloat16)
    rest = value - high.astype(jnp.float32)
    mid = rest.astype(jnp.bfloat16)
    low = (rest - mid.astype(jnp.float32)).astype(jnp.bfloat16)
    return high, mid, low


def iota(shape, dim):
    return lax.broadcasted_iota(jnp.int32, shape, dim)


def dot(left, right):
    return jnp.dot(left, right, preferred_element_type=jnp.float32)


def dot_t(left, right):
    return lax.dot_general(left, right, (((1,), (1,)), ((), ())), preferred_element_type=jnp.float32)


def fold(scores):
    rows, columns = scores.shape
    return jnp.max(scores.reshape(rows // 8, 8, columns), axis=0)


def column(tags, index):
    return jnp.transpose(tags)[:, index : index + 1]


class Place:
    def __init__(self):
        group = lax.axis_index("group")
        member = lax.axis_index("member")
        y, z = group // SIDE, group % SIDE
        x, self.core = member // 2, member % 2
        self.ys = [y] + [(y + d) % SIDE for d in range(1, SIDE)]
        self.zs = [z] + [(z + d) % SIDE for d in range(1, SIDE)]
        self.xs = [x] + [(x + d) % SIDE for d in range(1, SIDE)]
        self.y, self.z, self.x = y, z, x
        self.cell = group * SIDE + x
        self.sum = (y + z + x) % SIDE
        self.sums = [self.sum] + [(self.sum + d) % SIDE for d in range(1, SIDE)]
        self.source = self.sum * 16 + group
        self.halves = [value // 2 for value in self.ys]
        self.sibling = {"group": group, "member": x * 2 + 1 - self.core}

    def at(self, dy, dz, dx):
        return {"group": self.ys[dy] * SIDE + self.zs[dz], "member": self.xs[dx] * 2 + self.core}

    def cell_at(self, dy, dz, dx):
        return (self.ys[dy] * SIDE + self.zs[dz]) * SIDE + self.xs[dx]

    def eight_at(self, dy, dz, dx):
        return self.sums[(dy + dz + dx) % SIDE] * 2 + self.halves[dy]


def offsets(phase):
    return [(dy, dz, (phase - dy - dz) % SIDE) for dy in range(SIDE) for dz in range(SIDE)]


def mixed(phase):
    pairs = sorted(enumerate(offsets(phase)), key=lambda pair: hops(pair[1]))
    return [pair for both in zip(pairs[:8], pairs[:7:-1]) for pair in both]


def hops(offset):
    return sum(min(d, SIDE - d) for d in offset)


OTHERS = sorted(
    [offset for phase in range(SIDE) for offset in offsets(phase)][1:],
    key=lambda offset: -hops(offset),
)


def wait_for(ref, sem):
    pltpu.make_async_copy(ref, ref, sem).wait()


def greet(place):
    barrier = pltpu.get_barrier_semaphore()
    plane = [(dy, dz, 0) for dy in range(SIDE) for dz in range(SIDE)][1:]
    for offset in plane + [(0, 0, d) for d in range(1, SIDE)]:
        pl.semaphore_signal(barrier, inc=1, device_id=place.at(*offset), device_id_type=MESH)
    pl.semaphore_signal(barrier, inc=1, device_id=place.sibling, device_id_type=MESH)
    return barrier


def regroup(place, s):
    load = [
        pltpu.make_async_copy(src, dst, s.load_sems.at[n])
        for n, (src, dst) in enumerate(
            ((s.dest_hbm, s.dest), (s.cluster_hbm, s.cluster), (s.embed_hbm, s.embed))
        )
    ]
    for copy in load:
        copy.start()
    barrier = greet(place)
    load[0].wait()
    load[1].wait()

    rows = s.dest.shape[1]
    team = lax.shift_right_logical(s.dest[...], 3)
    cluster = s.cluster[...]
    in_team = (iota((16, rows), 0) == team).astype(jnp.float32)
    cells = jnp.concatenate(
        [in_team * (cluster == c).astype(jnp.float32) for c in range(4)], axis=0
    )
    earlier = (iota((rows, rows), 0) < iota((rows, rows), 1)).astype(jnp.bfloat16)
    rank = jnp.sum(cells * dot(cells.astype(jnp.bfloat16), earlier), axis=0, keepdims=True)
    counts = jnp.minimum(jnp.sum(cells, axis=1, keepdims=True), float(CELL))
    over = rank >= float(CELL)
    over_team = in_team * over.astype(jnp.float32)
    order = jnp.sum(
        over_team * dot(over_team.astype(jnp.bfloat16), earlier), axis=0, keepdims=True
    )
    filled = [
        jnp.sum(in_team * counts[16 * c : 16 * c + 16], axis=0, keepdims=True) for c in range(4)
    ]
    free0 = CELL - filled[0]
    free1 = free0 + CELL - filled[1]
    free2 = free1 + CELL - filled[2]
    chip = (
        (order >= free0).astype(jnp.int32)
        + (order >= free1).astype(jnp.int32)
        + (order >= free2).astype(jnp.int32)
    )
    spot = jnp.where(
        chip == 0,
        filled[0] + order,
        jnp.where(
            chip == 1,
            filled[1] + order - free0,
            jnp.where(chip == 2, filled[2] + order - free1, filled[3] + order - free2),
        ),
    )
    chip = jnp.where(over, chip, cluster)
    spot = jnp.where(over, spot, rank).astype(jnp.int32)
    cell = team * 4 + chip
    dy = lax.rem(lax.shift_right_logical(team, 2) + (SIDE - place.y), SIDE)
    dz = lax.rem(lax.rem(team, SIDE) + (SIDE - place.z), SIDE)
    dx = lax.rem(chip + (SIDE - place.x), SIDE)
    slot = lax.rem(dy + dz + dx, SIDE) * QUARTER + (dy * SIDE + dz) * CELL + spot
    lane = spot + (place.source % 8) * CELL

    pl.semaphore_wait(barrier, 19)
    for d in range(1, SIDE):
        device = place.at(0, 0, d)
        pl.semaphore_signal(s.plane_sem, inc=1, device_id=device, device_id_type=MESH)

    load[2].wait()

    send, left = s.send, s.left

    def landing(index):
        return pl.ds(pl.multiple_of(index * CELL, CELL), CELL)

    for phase in range(SIDE):
        base = phase * QUARTER
        chosen = (iota((QUARTER, rows), 0) + base == slot).astype(jnp.bfloat16)
        values = dot(chosen, s.embed[...])
        norm = jnp.sum(values * values, axis=1, keepdims=True)
        unit = (values * lax.rsqrt(norm + 1e-06)).astype(jnp.bfloat16)
        send[base : base + QUARTER] = unit
        if phase == 0:
            pl.semaphore_wait(s.plane_sem, 3)
            pltpu.make_async_copy(
                send.at[pl.ds(0, CELL)], left.at[landing(place.source)], s.recv_sems.at[0]
            ).start()

        for index, offset in mixed(phase):
            if any(offset):
                pltpu.make_async_remote_copy(
                    src_ref=send.at[landing(phase * 16 + index)],
                    dst_ref=left.at[landing(place.source)],
                    send_sem=s.send_sems.at[0],
                    recv_sem=s.recv_sems.at[phase],
                    device_id=place.at(*offset),
                    device_id_type=MESH,
                ).start()
        if phase == META_AFTER:
            in_cell = (iota((CELLS, rows), 0) == cell).astype(jnp.float32)
            at_lane = (iota((LANES, rows), 0) == lane).astype(jnp.bfloat16)
            labels = (in_cell * (cluster + 1).astype(jnp.float32)).astype(jnp.bfloat16)
            s.meta[...] = dot_t(labels, at_lane).reshape(CELLS, 1, LANES)
            send_labels(place, s)
    return in_cell, at_lane, team, cluster, chip, lane


def send_labels(place, s):
    for offset in OTHERS:
        pltpu.make_async_remote_copy(
            src_ref=s.meta.at[pl.ds(place.cell_at(*offset), 1)],
            dst_ref=s.meta_in.at[pl.ds(place.source, 1)],
            send_sem=s.send_sems.at[1],
            recv_sem=s.meta_sem,
            device_id=place.at(*offset),
            device_id_type=MESH,
        ).start()
    pltpu.make_async_copy(
        s.meta.at[pl.ds(place.cell, 1)], s.meta_in.at[pl.ds(place.source, 1)], s.meta_sem
    ).start()


def quarter(place, phase):
    if isinstance(phase, int):
        return place.sums[-phase % SIDE]
    return (place.sum + SIDE - phase) % SIDE


def rows_of(index):
    return pl.ds(pl.multiple_of(index * QUARTER, QUARTER), QUARTER)


def arrived(place, phase):
    return rows_of(quarter(place, phase))


def to_sources(place, source_ref, dest_ref, size, send_sem, recv_sem):
    for offset in OTHERS:
        pltpu.make_async_remote_copy(
            src_ref=source_ref.at[pl.ds(place.eight_at(*offset) * size, size)],
            dst_ref=dest_ref.at[pl.ds(place.cell * size, size)],
            send_sem=send_sem,
            recv_sem=recv_sem,
            device_id=place.at(*offset),
            device_id_type=MESH,
        ).start()
    pltpu.make_async_copy(
        source_ref.at[pl.ds(place.source // 8 * size, size)],
        dest_ref.at[pl.ds(place.cell * size, size)],
        recv_sem,
    ).start()


def wait_sent(s):
    sent = pl.ds(0, SLOTS - CELL)
    wait_for(s.send.at[sent], s.send_sems.at[0])
    sent = pl.ds(0, CELLS - 1)
    wait_for(s.meta.at[sent], s.send_sems.at[1])


def team_kernel(names, *refs):
    s = types.SimpleNamespace(**dict(zip(names, refs)))
    place = Place()
    in_cell, at_lane, team, cluster, chip, lane = regroup(place, s)
    left, other = s.left, s.other
    left[SLOTS + FORWARD :] = jnp.zeros((LEFT_SPILL - FORWARD, left.shape[1]), jnp.bfloat16)

    def to_pair(src, dst, index):
        copy = pltpu.make_async_remote_copy(
            src_ref=src,
            dst_ref=dst,
            send_sem=s.pair_sems.at[0, index],
            recv_sem=s.pair_sems.at[1, index],
            device_id=place.sibling,
            device_id_type=MESH,
        )
        copy.start()
        return copy

    wait_for(s.meta_in, s.meta_sem)
    label = jnp.sum(s.meta_in[...].reshape(8, 8, LANES), axis=1)
    own = (place.x + 1).astype(jnp.float32)
    below = (iota((LANES, LANES), 0) < iota((LANES, LANES), 1)).astype(jnp.bfloat16)
    hits = [
        (label == (lax.rem(place.x + d, SIDE) + 1).astype(jnp.float32)).astype(jnp.float32)
        for d in range(1, SIDE)
    ]
    hit = jnp.concatenate(hits, axis=0)
    within = dot(hit.astype(jnp.bfloat16), below)
    totals = jnp.sum(hit, axis=1, keepdims=True)
    places = jnp.full((8, LANES), -1.0, jnp.float32)
    worst = jnp.zeros((1, 1), jnp.float32)
    row, col = iota((8, 8), 0), iota((8, 8), 1)
    for d in range(3):
        total = totals[8 * d : 8 * d + 8]
        spread = jnp.broadcast_to(total, (8, 8))
        before = jnp.sum(jnp.where(row < col, spread, 0.0), axis=0, keepdims=True)
        spread = jnp.broadcast_to(before, (8, 8))
        before = jnp.sum(jnp.where(row == col, spread, 0.0), axis=1, keepdims=True)
        position = within[8 * d : 8 * d + 8] + before
        places = jnp.where(
            (hits[d] > 0.0) & (position < float(SPILL)), position + float(SPILL * d), places
        )
        worst = jnp.maximum(worst, jnp.sum(total, axis=0, keepdims=True))
    failed = jnp.broadcast_to((worst > float(SPILL)).astype(jnp.float32), (8, LANES))
    s.label_out[0:8] = label
    s.label_out[8:16] = failed
    copy_label = to_pair(s.label_out, s.label_in, 4)
    s.places_out[...] = places.reshape(8, 1, LANES)
    to_sources(place, s.places_out, s.places_in, 1, s.send_sems.at[2], s.places_sem)
    select, forward = s.select, s.forward
    for q in range(8):
        select[q // 2, :, (q % 2) * LANES : (q % 2 + 1) * LANES] = (
            iota((FORWARD, LANES), 0).astype(jnp.float32) == places[q : q + 1]
        ).astype(jnp.bfloat16)
    taken = jnp.zeros((FORWARD, 1), jnp.float32)
    for q in range(SIDE):
        taken = taken + jnp.sum(select[q].astype(jnp.float32), axis=1, keepdims=True)
    mark = jnp.where((iota((FORWARD, LANES), 1) == 0) & (taken < 0.5), EMPTY, 0.0)
    s.moved[...] = jnp.zeros(s.moved.shape, jnp.float32)
    s.moved[:, 0:LANES] = mark
    s.best[...] = jnp.full(s.best.shape, NONE, jnp.float32)

    def set_bias(ref, tags):
        for q in range(8):
            ref[q * LANES : (q + 1) * LANES, 0:1] = jnp.where(column(tags, q) == own, 0.0, NONE)

    bias, other_bias = s.bias, s.other_bias
    set_bias(bias, label)
    copy_label.wait()
    set_bias(other_bias, s.label_in[0:8])

    def block(right, right_bias, index, target, same=False):
        part = rows_of(index)
        scores = dot_t(right[part], left[rows_of(target)]) + right_bias[part, 0:1]
        if same:
            shape = (QUARTER, QUARTER)
            scores = jnp.where(iota(shape, 0) == iota(shape, 1), NONE, scores)
        s.best[target] = jnp.maximum(s.best[target], fold(scores))

    def blocks(right, right_bias, phase, same):
        last = quarter(place, phase)
        block(right, right_bias, last, last, same)

        def one(index, carry):
            first = quarter(place, index)
            block(right, right_bias, last, first)
            block(right, right_bias, first, last)
            return carry

        lax.fori_loop(0, phase, one, 0)

    shared = []
    for phase in range(SIDE):
        part = arrived(place, phase)
        wait_for(left.at[part], s.recv_sems.at[phase])
        shared.append(to_pair(left.at[part], other.at[part], phase))
        s.moved[...] += dot(select[quarter(place, phase)], left[part])
        if phase < SIDE - 1:
            blocks(left, bias, phase, True)
            if phase > 0:
                shared[phase - 1].wait()
                blocks(other, other_bias, phase - 1, False)

    forward[...] = s.moved[...].astype(jnp.bfloat16)
    to_line = []
    for d in SPILL_ORDER:
        copy = pltpu.make_async_remote_copy(
            src_ref=forward.at[pl.ds(d * SPILL, SPILL)],
            dst_ref=left.at[pl.ds(SLOTS + d * SPILL, SPILL)],
            send_sem=s.spill_sems.at[0, d],
            recv_sem=s.spill_sems.at[1, d],
            device_id=place.at(0, 0, d + 1),
            device_id_type=MESH,
        )
        copy.start()
        to_line.append(copy)
    blocks(left, bias, SIDE - 1, True)
    for phase in (SIDE - 2, SIDE - 1):
        shared[phase].wait()
        blocks(other, other_bias, phase, False)

    rows = cluster.shape[1]
    wait_for(s.places_in, s.places_sem)
    held = dot(s.places_in[...].reshape(CELLS, LANES).astype(jnp.bfloat16), at_lane)
    held = jnp.sum(held * in_cell, axis=0, keepdims=True).astype(jnp.int32)
    straight = chip == cluster
    entry = ENTRY * (team * 4 + cluster) + jnp.where(
        straight, 0, 1 + (held >= LANES).astype(jnp.int32)
    )
    in_entry = (iota((ENTRY * CELLS, rows), 0) == entry).astype(jnp.float32)
    spot = jnp.where(straight, lane, jnp.where(held >= LANES, held - LANES, held))
    at_spot = (iota((LANES, rows), 0) == spot).astype(jnp.bfloat16)

    spill_pair = []
    for d, copy in zip(SPILL_ORDER, to_line):
        copy.wait()
        part = pl.ds(d * SPILL, SPILL)
        spill_pair.append(
            to_pair(left.at[pl.ds(SLOTS + d * SPILL, SPILL)], s.other_spill.at[part], 5 + d)
        )

    def against(right, right_bias, best):
        def one(index, best):
            part = rows_of(index)
            scores = dot_t(right[part], left[SLOTS:]) + right_bias[part, 0:1]
            return jnp.maximum(best, fold(scores))

        return lax.fori_loop(0, SIDE, one, best)

    def against_spill(right, same):
        scores = dot_t(right, left[...]) + jnp.where(
            right[:, 0:1].astype(jnp.float32) > 1.5, NONE, 0.0
        )
        if same:
            scores = jnp.where(
                iota(scores.shape, 0) + SLOTS == iota(scores.shape, 1), NONE, scores
            )
        return fold(scores)

    best_spill = jnp.full((8, LEFT_SPILL), NONE, jnp.float32)
    best_spill = against(left, bias, best_spill)
    best_spill = against(other, other_bias, best_spill)
    best_all = against_spill(left[SLOTS : SLOTS + FORWARD], True)
    for copy in spill_pair:
        copy.wait()
    best_all = jnp.maximum(best_all, against_spill(s.other_spill[...], False))
    best_spill = jnp.max(jnp.maximum(best_spill, best_all[:, SLOTS:]), axis=0, keepdims=True)

    failed = jnp.maximum(failed, s.label_in[8:16])[0:1]
    best_out = s.best_out
    for q in range(8):
        half = slice((q % 2) * LANES, (q % 2 + 1) * LANES)
        part = jnp.maximum(s.best[q // 2, :, half], best_all[:, q * LANES : (q + 1) * LANES])
        part = jnp.max(part, axis=0, keepdims=True)
        best_out[q * ENTRY] = jnp.where(failed > 0.0, FAILED, part)
        for half in range(LEFT_SPILL // LANES):
            best_out[q * ENTRY + 1 + half] = best_spill[:, half * LANES : (half + 1) * LANES]
    to_sources(place, best_out, s.best_in, ENTRY, s.send_sems.at[3], s.best_sem)
    wait_sent(s)
    wait_for(s.places_in.at[pl.ds(0, CELLS - 1)], s.send_sems.at[2])
    wait_for(s.best_in, s.best_sem)
    found = s.best_in[...].reshape(ENTRY * CELLS, LANES)
    worst = jnp.max(jnp.max(found, axis=0, keepdims=True), axis=1, keepdims=True)
    picked = sum(dot(piece, at_spot) for piece in split3(found))
    score = jnp.maximum(jnp.sum(picked * in_entry, axis=0, keepdims=True), -1.0)
    s.out[...] = jnp.where(worst > 4.0, FAILED, score)

    wait_for(s.best_in.at[pl.ds(0, ENTRY * (CELLS - 1))], s.send_sems.at[3])


def general_kernel(names, *refs):
    s = types.SimpleNamespace(**dict(zip(names, refs)))
    place = Place()
    in_cell, at_lane, *_ = regroup(place, s)
    left = s.left
    for phase in range(SIDE):
        wait_for(left.at[arrived(place, phase)], s.recv_sems.at[phase])
    wait_for(s.meta_in, s.meta_sem)
    label = jnp.sum(s.meta_in[...].reshape(8, 8, LANES), axis=1)
    s.label_out[...] = label
    copies = []
    for block in range(1, 8):
        for index, (src, dst) in enumerate(((left, s.gather), (s.label_out, s.tags))):
            copy = pltpu.make_async_remote_copy(
                src_ref=src,
                dst_ref=dst.at[block - 1],
                send_sem=s.line_sems.at[0, index, block - 1],
                recv_sem=s.line_sems.at[1, index, block - 1],
                device_id={"member": place.xs[block // 2] * 2 + (place.core + block) % 2},
                device_id_type=MESH,
            )
            copy.start()
            copies.append(copy)
    left_label = jnp.concatenate([label[q : q + 1] for q in range(8)], axis=1)

    def against(right, tags, same):
        for q in range(8):
            s.bias[q * LANES : (q + 1) * LANES, 0:1] = column(tags, q)

        def one(index, best):
            base = pl.multiple_of(index * QUARTER, QUARTER)
            part = pl.ds(base, QUARTER)
            scores = dot_t(right[part], left[...])
            counts = s.bias[part, 0:1] == left_label
            if same:
                shape = (QUARTER, SLOTS)
                counts = counts & (iota(shape, 0) + base != iota(shape, 1))
            return jnp.maximum(best, fold(jnp.where(counts, scores, NONE)))

        start = jnp.full((8, SLOTS), NONE, jnp.float32)
        return lax.fori_loop(0, SLOTS // QUARTER, one, start)

    best = against(left, label, True)
    for copy in copies:
        copy.wait()

    def block(index, best):
        return jnp.maximum(best, against(s.gather.at[index], s.tags[index], False))

    best = jnp.max(lax.fori_loop(0, 7, block, best), axis=0, keepdims=True)
    for q in range(8):
        s.best_out[q] = best[:, q * LANES : (q + 1) * LANES]
    to_sources(place, s.best_out, s.best_in, 1, s.send_sems.at[2], s.best_sem)
    wait_for(s.best_in, s.best_sem)
    found = s.best_in[...].reshape(CELLS, LANES)
    score = sum(dot(piece, at_lane) for piece in split3(found))
    s.out[...] = jnp.maximum(jnp.sum(score * in_cell, axis=0, keepdims=True), -1.0)
    wait_sent(s)
    wait_for(s.best_in.at[pl.ds(0, CELLS - 1)], s.send_sems.at[2])


def call(kernel, name, collective, extra, embed, destination, cluster):
    rows, features = embed.shape
    bf16, f32, i32 = jnp.bfloat16, jnp.float32, jnp.int32
    vmem, dma = pltpu.VMEM, pltpu.SemaphoreType.DMA
    scratch = dict(
        dest=vmem((1, rows), i32),
        cluster=vmem((1, rows), i32),
        embed=vmem((rows, features), bf16),
        send=vmem((SLOTS, features), bf16),
        meta=vmem((CELLS, 1, LANES), f32),
        meta_in=vmem((CELLS, 1, LANES), f32),
        bias=vmem((SLOTS, LANES), f32),
        plane_sem=pltpu.SemaphoreType.REGULAR,
        load_sems=dma((3,)),
        send_sems=dma((4,)),
        recv_sems=dma((SIDE,)),
        meta_sem=dma,
        best_sem=dma,
        **extra(features),
    )
    names = ("dest_hbm", "cluster_hbm", "embed_hbm", "out", *scratch)
    return pl.pallas_call(
        functools.partial(kernel, names),
        out_shape=jax.ShapeDtypeStruct((1, rows), f32),
        in_specs=[pl.BlockSpec(memory_space=pl.ANY)] * 3,
        out_specs=pl.BlockSpec(memory_space=pltpu.VMEM),
        scratch_shapes=list(scratch.values()),
        compiler_params=pltpu.CompilerParams(
            collective_id=collective, has_side_effects=True, vmem_limit_bytes=40 * 2**20
        ),
        name=name,
    )(destination.reshape(1, rows), cluster.reshape(1, rows), embed)


def team_scratch(features):
    bf16, f32, vmem, dma = jnp.bfloat16, jnp.float32, pltpu.VMEM, pltpu.SemaphoreType.DMA
    return dict(
        left=vmem((SLOTS + LEFT_SPILL, features), bf16),
        other=vmem((SLOTS, features), bf16),
        other_spill=vmem((FORWARD, features), bf16),
        select=vmem((SIDE, FORWARD, QUARTER), bf16),
        moved=vmem((FORWARD, features), f32),
        best=vmem((SIDE, 8, QUARTER), f32),
        forward=vmem((FORWARD, features), bf16),
        label_out=vmem((16, LANES), f32),
        label_in=vmem((16, LANES), f32),
        other_bias=vmem((SLOTS, LANES), f32),
        places_out=vmem((8, 1, LANES), f32),
        places_in=vmem((CELLS, 1, LANES), f32),
        best_out=vmem((8 * ENTRY, 1, LANES), f32),
        best_in=vmem((CELLS * ENTRY, 1, LANES), f32),
        places_sem=dma,
        pair_sems=dma((2, 8)),
        spill_sems=dma((2, 3)),
    )


def general_scratch(features):
    bf16, f32, vmem, dma = jnp.bfloat16, jnp.float32, pltpu.VMEM, pltpu.SemaphoreType.DMA
    return dict(
        left=vmem((SLOTS, features), bf16),
        gather=vmem((7, SLOTS, features), bf16),
        label_out=vmem((8, LANES), f32),
        tags=vmem((7, 8, LANES), f32),
        best_out=vmem((8, 1, LANES), f32),
        best_in=vmem((CELLS, 1, LANES), f32),
        line_sems=dma((2, 2, 7)),
    )


def shards(embed, destination, cluster):
    rows = embed.shape[0]
    scores = call(team_kernel, "team_scores", 0, team_scratch, embed, destination, cluster)

    def general(*args):
        return call(general_kernel, "general_scores", 1, general_scratch, *args).reshape(rows)

    return lax.cond(
        scores[0, 0] > 4.0,
        general,
        lambda *unused: scores.reshape(rows),
        embed,
        destination,
        cluster,
    )


def solution(mesh):
    in_specs = (P(("group", "member"), None), P(("group", "member")), P(("group", "member")))
    out_specs = P(("group", "member"))
    return jax.shard_map(shards, mesh=mesh, in_specs=in_specs, out_specs=out_specs, check_vma=False)
```

```python
import functools
import types

import jax
import jax.numpy as jnp
from jax import lax
from jax.experimental import pallas as pl
from jax.experimental.pallas import tpu as pltpu
from jax.sharding import PartitionSpec as P

MESH = pl.DeviceIdType.MESH
SIDE = 4
CELLS = 64
CELL = 16
SPILL = 80
LANES = 128
QUARTER = 256
SLOTS = CELLS * CELL
FORWARD = 3 * SPILL
LEFT_SPILL = 256
NONE = -4.0
META_AFTER = 0
ENTRY = 3
FAILED = 8.0
EMPTY = 2.0
SPILL_ORDER = (1, 0, 2)


def split3(value):
    high = value.astype(jnp.bfloat16)
    rest = value - high.astype(jnp.float32)
    mid = rest.astype(jnp.bfloat16)
    low = (rest - mid.astype(jnp.float32)).astype(jnp.bfloat16)
    return high, mid, low


def iota(shape, dim):
    return lax.broadcasted_iota(jnp.int32, shape, dim)


def dot(left, right):
    return jnp.dot(left, right, preferred_element_type=jnp.float32)


def dot_t(left, right):
    return lax.dot_general(left, right, (((1,), (1,)), ((), ())), preferred_element_type=jnp.float32)


def fold(scores):
    rows, columns = scores.shape
    return jnp.max(scores.reshape(rows // 8, 8, columns), axis=0)


def column(tags, index):
    return jnp.transpose(tags)[:, index : index + 1]


class Place:
    def __init__(self):
        group = lax.axis_index("group")
        member = lax.axis_index("member")
        y, z = group // SIDE, group % SIDE
        x, self.core = member // 2, member % 2
        self.ys = [y] + [(y + d) % SIDE for d in range(1, SIDE)]
        self.zs = [z] + [(z + d) % SIDE for d in range(1, SIDE)]
        self.xs = [x] + [(x + d) % SIDE for d in range(1, SIDE)]
        self.y, self.z, self.x = y, z, x
        self.cell = group * SIDE + x
        self.sum = (y + z + x) % SIDE
        self.sums = [self.sum] + [(self.sum + d) % SIDE for d in range(1, SIDE)]
        self.source = self.sum * 16 + group
        self.halves = [value // 2 for value in self.ys]
        self.sibling = {"group": group, "member": x * 2 + 1 - self.core}

    def at(self, dy, dz, dx):
        return {"group": self.ys[dy] * SIDE + self.zs[dz], "member": self.xs[dx] * 2 + self.core}

    def cell_at(self, dy, dz, dx):
        return (self.ys[dy] * SIDE + self.zs[dz]) * SIDE + self.xs[dx]

    def eight_at(self, dy, dz, dx):
        return self.sums[(dy + dz + dx) % SIDE] * 2 + self.halves[dy]


def offsets(phase):
    return [(dy, dz, (phase - dy - dz) % SIDE) for dy in range(SIDE) for dz in range(SIDE)]


def mixed(phase):
    pairs = sorted(enumerate(offsets(phase)), key=lambda pair: hops(pair[1]))
    return [pair for both in zip(pairs[:8], pairs[:7:-1]) for pair in both]


def hops(offset):
    return sum(min(d, SIDE - d) for d in offset)


OTHERS = sorted(
    [offset for phase in range(SIDE) for offset in offsets(phase)][1:],
    key=lambda offset: -hops(offset),
)


def wait_for(ref, sem):
    pltpu.make_async_copy(ref, ref, sem).wait()


def greet(place):
    barrier = pltpu.get_barrier_semaphore()
    plane = [(dy, dz, 0) for dy in range(SIDE) for dz in range(SIDE)][1:]
    for offset in plane + [(0, 0, d) for d in range(1, SIDE)]:
        pl.semaphore_signal(barrier, inc=1, device_id=place.at(*offset), device_id_type=MESH)
    pl.semaphore_signal(barrier, inc=1, device_id=place.sibling, device_id_type=MESH)
    return barrier


def regroup(place, s):
    load = [
        pltpu.make_async_copy(src, dst, s.load_sems.at[n])
        for n, (src, dst) in enumerate(
            ((s.dest_hbm, s.dest), (s.cluster_hbm, s.cluster), (s.embed_hbm, s.embed))
        )
    ]
    for copy in load:
        copy.start()
    barrier = greet(place)
    load[0].wait()
    load[1].wait()

    rows = s.dest.shape[1]
    team = lax.shift_right_logical(s.dest[...], 3)
    cluster = s.cluster[...]
    in_team = (iota((16, rows), 0) == team).astype(jnp.float32)
    cells = jnp.concatenate(
        [in_team * (cluster == c).astype(jnp.float32) for c in range(4)], axis=0
    )
    earlier = (iota((rows, rows), 0) < iota((rows, rows), 1)).astype(jnp.bfloat16)
    rank = jnp.sum(cells * dot(cells.astype(jnp.bfloat16), earlier), axis=0, keepdims=True)
    counts = jnp.minimum(jnp.sum(cells, axis=1, keepdims=True), float(CELL))
    over = rank >= float(CELL)
    over_team = in_team * over.astype(jnp.float32)
    order = jnp.sum(
        over_team * dot(over_team.astype(jnp.bfloat16), earlier), axis=0, keepdims=True
    )
    filled = [
        jnp.sum(in_team * counts[16 * c : 16 * c + 16], axis=0, keepdims=True) for c in range(4)
    ]
    free0 = CELL - filled[0]
    free1 = free0 + CELL - filled[1]
    free2 = free1 + CELL - filled[2]
    chip = (
        (order >= free0).astype(jnp.int32)
        + (order >= free1).astype(jnp.int32)
        + (order >= free2).astype(jnp.int32)
    )
    spot = jnp.where(
        chip == 0,
        filled[0] + order,
        jnp.where(
            chip == 1,
            filled[1] + order - free0,
            jnp.where(chip == 2, filled[2] + order - free1, filled[3] + order - free2),
        ),
    )
    chip = jnp.where(over, chip, cluster)
    spot = jnp.where(over, spot, rank).astype(jnp.int32)
    cell = team * 4 + chip
    dy = lax.rem(lax.shift_right_logical(team, 2) + (SIDE - place.y), SIDE)
    dz = lax.rem(lax.rem(team, SIDE) + (SIDE - place.z), SIDE)
    dx = lax.rem(chip + (SIDE - place.x), SIDE)
    slot = lax.rem(dy + dz + dx, SIDE) * QUARTER + (dy * SIDE + dz) * CELL + spot
    lane = spot + (place.source % 8) * CELL

    pl.semaphore_wait(barrier, 19)
    for d in range(1, SIDE):
        device = place.at(0, 0, d)
        pl.semaphore_signal(s.plane_sem, inc=1, device_id=device, device_id_type=MESH)

    load[2].wait()

    send, left = s.send, s.left

    def landing(index):
        return pl.ds(pl.multiple_of(index * CELL, CELL), CELL)

    for phase in range(SIDE):
        base = phase * QUARTER
        chosen = (iota((QUARTER, rows), 0) + base == slot).astype(jnp.bfloat16)
        values = dot(chosen, s.embed[...])
        norm = jnp.sum(values * values, axis=1, keepdims=True)
        unit = (values * lax.rsqrt(norm + 1e-06)).astype(jnp.bfloat16)
        send[base : base + QUARTER] = unit
        if phase == 0:
            pl.semaphore_wait(s.plane_sem, 3)
            pltpu.make_async_copy(
                send.at[pl.ds(0, CELL)], left.at[landing(place.source)], s.recv_sems.at[0]
            ).start()

        for index, offset in mixed(phase):
            if any(offset):
                pltpu.make_async_remote_copy(
                    src_ref=send.at[landing(phase * 16 + index)],
                    dst_ref=left.at[landing(place.source)],
                    send_sem=s.send_sems.at[0],
                    recv_sem=s.recv_sems.at[phase],
                    device_id=place.at(*offset),
                    device_id_type=MESH,
                ).start()
        if phase == META_AFTER:
            in_cell = (iota((CELLS, rows), 0) == cell).astype(jnp.float32)
            at_lane = (iota((LANES, rows), 0) == lane).astype(jnp.bfloat16)
            labels = (in_cell * (cluster + 1).astype(jnp.float32)).astype(jnp.bfloat16)
            s.meta[...] = dot_t(labels, at_lane).reshape(CELLS, 1, LANES)
            send_labels(place, s)
    return in_cell, at_lane, team, cluster, chip, lane


def send_labels(place, s):
    for offset in OTHERS:
        pltpu.make_async_remote_copy(
            src_ref=s.meta.at[pl.ds(place.cell_at(*offset), 1)],
            dst_ref=s.meta_in.at[pl.ds(place.source, 1)],
            send_sem=s.send_sems.at[1],
            recv_sem=s.meta_sem,
            device_id=place.at(*offset),
            device_id_type=MESH,
        ).start()
    pltpu.make_async_copy(
        s.meta.at[pl.ds(place.cell, 1)], s.meta_in.at[pl.ds(place.source, 1)], s.meta_sem
    ).start()


def quarter(place, phase):
    if isinstance(phase, int):
        return place.sums[-phase % SIDE]
    return (place.sum + SIDE - phase) % SIDE


def rows_of(index):
    return pl.ds(pl.multiple_of(index * QUARTER, QUARTER), QUARTER)


def arrived(place, phase):
    return rows_of(quarter(place, phase))


def to_sources(place, source_ref, dest_ref, size, send_sem, recv_sem):
    for offset in OTHERS:
        pltpu.make_async_remote_copy(
            src_ref=source_ref.at[pl.ds(place.eight_at(*offset) * size, size)],
            dst_ref=dest_ref.at[pl.ds(place.cell * size, size)],
            send_sem=send_sem,
            recv_sem=recv_sem,
            device_id=place.at(*offset),
            device_id_type=MESH,
        ).start()
    pltpu.make_async_copy(
        source_ref.at[pl.ds(place.source // 8 * size, size)],
        dest_ref.at[pl.ds(place.cell * size, size)],
        recv_sem,
    ).start()


def wait_sent(s):
    sent = pl.ds(0, SLOTS - CELL)
    wait_for(s.send.at[sent], s.send_sems.at[0])
    sent = pl.ds(0, CELLS - 1)
    wait_for(s.meta.at[sent], s.send_sems.at[1])


def team_kernel(names, *refs):
    s = types.SimpleNamespace(**dict(zip(names, refs)))
    place = Place()
    in_cell, at_lane, team, cluster, chip, lane = regroup(place, s)
    left, other = s.left, s.other
    left[SLOTS + FORWARD :] = jnp.zeros((LEFT_SPILL - FORWARD, left.shape[1]), jnp.bfloat16)

    def to_pair(src, dst, index):
        copy = pltpu.make_async_remote_copy(
            src_ref=src,
            dst_ref=dst,
            send_sem=s.pair_sems.at[0, index],
            recv_sem=s.pair_sems.at[1, index],
            device_id=place.sibling,
            device_id_type=MESH,
        )
        copy.start()
        return copy

    wait_for(s.meta_in, s.meta_sem)
    label = jnp.sum(s.meta_in[...].reshape(8, 8, LANES), axis=1)
    own = (place.x + 1).astype(jnp.float32)
    below = (iota((LANES, LANES), 0) < iota((LANES, LANES), 1)).astype(jnp.bfloat16)
    hits = [
        (label == (lax.rem(place.x + d, SIDE) + 1).astype(jnp.float32)).astype(jnp.float32)
        for d in range(1, SIDE)
    ]
    hit = jnp.concatenate(hits, axis=0)
    within = dot(hit.astype(jnp.bfloat16), below)
    totals = jnp.sum(hit, axis=1, keepdims=True)
    places = jnp.full((8, LANES), -1.0, jnp.float32)
    worst = jnp.zeros((1, 1), jnp.float32)
    row, col = iota((8, 8), 0), iota((8, 8), 1)
    for d in range(3):
        total = totals[8 * d : 8 * d + 8]
        spread = jnp.broadcast_to(total, (8, 8))
        before = jnp.sum(jnp.where(row < col, spread, 0.0), axis=0, keepdims=True)
        spread = jnp.broadcast_to(before, (8, 8))
        before = jnp.sum(jnp.where(row == col, spread, 0.0), axis=1, keepdims=True)
        position = within[8 * d : 8 * d + 8] + before
        places = jnp.where(
            (hits[d] > 0.0) & (position < float(SPILL)), position + float(SPILL * d), places
        )
        worst = jnp.maximum(worst, jnp.sum(total, axis=0, keepdims=True))
    failed = jnp.broadcast_to((worst > float(SPILL)).astype(jnp.float32), (8, LANES))
    s.label_out[0:8] = label
    s.label_out[8:16] = failed
    copy_label = to_pair(s.label_out, s.label_in, 4)
    s.places_out[...] = places.reshape(8, 1, LANES)
    to_sources(place, s.places_out, s.places_in, 1, s.send_sems.at[2], s.places_sem)
    select, forward = s.select, s.forward
    for q in range(8):
        select[q // 2, :, (q % 2) * LANES : (q % 2 + 1) * LANES] = (
            iota((FORWARD, LANES), 0).astype(jnp.float32) == places[q : q + 1]
        ).astype(jnp.bfloat16)
    taken = jnp.zeros((FORWARD, 1), jnp.float32)
    for q in range(SIDE):
        taken = taken + jnp.sum(select[q].astype(jnp.float32), axis=1, keepdims=True)
    mark = jnp.where((iota((FORWARD, LANES), 1) == 0) & (taken < 0.5), EMPTY, 0.0)
    s.moved[...] = jnp.zeros(s.moved.shape, jnp.float32)
    s.moved[:, 0:LANES] = mark
    s.best[...] = jnp.full(s.best.shape, NONE, jnp.float32)

    def set_bias(ref, tags):
        for q in range(8):
            ref[q * LANES : (q + 1) * LANES, 0:1] = jnp.where(column(tags, q) == own, 0.0, NONE)

    bias, other_bias = s.bias, s.other_bias
    set_bias(bias, label)
    copy_label.wait()
    set_bias(other_bias, s.label_in[0:8])

    def block(right, right_bias, index, target, same=False):
        part = rows_of(index)
        scores = dot_t(right[part], left[rows_of(target)]) + right_bias[part, 0:1]
        if same:
            shape = (QUARTER, QUARTER)
            scores = jnp.where(iota(shape, 0) == iota(shape, 1), NONE, scores)
        s.best[target] = jnp.maximum(s.best[target], fold(scores))

    def blocks(right, right_bias, phase, same):
        last = quarter(place, phase)
        block(right, right_bias, last, last, same)

        def one(index, carry):
            first = quarter(place, index)
            block(right, right_bias, last, first)
            block(right, right_bias, first, last)
            return carry

        lax.fori_loop(0, phase, one, 0)

    shared = []
    for phase in range(SIDE):
        part = arrived(place, phase)
        wait_for(left.at[part], s.recv_sems.at[phase])
        shared.append(to_pair(left.at[part], other.at[part], phase))
        s.moved[...] += dot(select[quarter(place, phase)], left[part])
        if phase < SIDE - 1:
            blocks(left, bias, phase, True)
            if phase > 0:
                shared[phase - 1].wait()
                blocks(other, other_bias, phase - 1, False)

    forward[...] = s.moved[...].astype(jnp.bfloat16)
    to_line = []
    for d in SPILL_ORDER:
        copy = pltpu.make_async_remote_copy(
            src_ref=forward.at[pl.ds(d * SPILL, SPILL)],
            dst_ref=left.at[pl.ds(SLOTS + d * SPILL, SPILL)],
            send_sem=s.spill_sems.at[0, d],
            recv_sem=s.spill_sems.at[1, d],
            device_id=place.at(0, 0, d + 1),
            device_id_type=MESH,
        )
        copy.start()
        to_line.append(copy)
    blocks(left, bias, SIDE - 1, True)
    for phase in (SIDE - 2, SIDE - 1):
        shared[phase].wait()
        blocks(other, other_bias, phase, False)

    rows = cluster.shape[1]
    wait_for(s.places_in, s.places_sem)
    held = dot(s.places_in[...].reshape(CELLS, LANES).astype(jnp.bfloat16), at_lane)
    held = jnp.sum(held * in_cell, axis=0, keepdims=True).astype(jnp.int32)
    straight = chip == cluster
    entry = ENTRY * (team * 4 + cluster) + jnp.where(
        straight, 0, 1 + (held >= LANES).astype(jnp.int32)
    )
    in_entry = (iota((ENTRY * CELLS, rows), 0) == entry).astype(jnp.float32)
    spot = jnp.where(straight, lane, jnp.where(held >= LANES, held - LANES, held))
    at_spot = (iota((LANES, rows), 0) == spot).astype(jnp.bfloat16)

    spill_pair = []
    for d, copy in zip(SPILL_ORDER, to_line):
        copy.wait()
        part = pl.ds(d * SPILL, SPILL)
        spill_pair.append(
            to_pair(left.at[pl.ds(SLOTS + d * SPILL, SPILL)], s.other_spill.at[part], 5 + d)
        )

    def against(right, right_bias, best):
        return jnp.maximum(best, fold(dot_t(right[0:SLOTS], left[SLOTS:]) + right_bias[:, 0:1]))

    def against_spill(right, same):
        scores = dot_t(right, left[...]) + jnp.where(
            right[:, 0:1].astype(jnp.float32) > 1.5, NONE, 0.0
        )
        if same:
            scores = jnp.where(
                iota(scores.shape, 0) + SLOTS == iota(scores.shape, 1), NONE, scores
            )
        return fold(scores)

    best_all = against_spill(left[SLOTS : SLOTS + FORWARD], True)
    best_spill = against(other, other_bias, against(left, bias, best_all[:, SLOTS:]))
    for copy in spill_pair:
        copy.wait()
    best_all = jnp.maximum(best_all, against_spill(s.other_spill[...], False))
    best_spill = jnp.max(jnp.maximum(best_spill, best_all[:, SLOTS:]), axis=0, keepdims=True)

    failed = jnp.maximum(failed, s.label_in[8:16])[0:1]
    best_out = s.best_out
    best_main = jnp.concatenate([s.best[q] for q in range(SIDE)], axis=1)
    best_main = jnp.max(jnp.maximum(best_main, best_all[:, 0:SLOTS]), axis=0, keepdims=True)
    best_main = jnp.where(failed[0:1, 0:1] > 0.0, FAILED, best_main)
    for q in range(8):
        best_out[q * ENTRY] = best_main[:, q * LANES : (q + 1) * LANES]
        for half in range(LEFT_SPILL // LANES):
            best_out[q * ENTRY + 1 + half] = best_spill[:, half * LANES : (half + 1) * LANES]
    to_sources(place, best_out, s.best_in, ENTRY, s.send_sems.at[3], s.best_sem)
    wait_sent(s)
    wait_for(s.places_in.at[pl.ds(0, CELLS - 1)], s.send_sems.at[2])
    wait_for(s.best_in, s.best_sem)
    found = s.best_in[...].reshape(ENTRY * CELLS, LANES)
    worst = jnp.max(jnp.max(found, axis=0, keepdims=True), axis=1, keepdims=True)
    picked = sum(dot(piece, at_spot) for piece in split3(found))
    score = jnp.maximum(jnp.sum(picked * in_entry, axis=0, keepdims=True), -1.0)
    s.out[...] = jnp.where(worst > 4.0, FAILED, score)

    wait_for(s.best_in.at[pl.ds(0, ENTRY * (CELLS - 1))], s.send_sems.at[3])


def general_kernel(names, *refs):
    s = types.SimpleNamespace(**dict(zip(names, refs)))
    place = Place()
    in_cell, at_lane, *_ = regroup(place, s)
    left = s.left
    for phase in range(SIDE):
        wait_for(left.at[arrived(place, phase)], s.recv_sems.at[phase])
    wait_for(s.meta_in, s.meta_sem)
    label = jnp.sum(s.meta_in[...].reshape(8, 8, LANES), axis=1)
    s.label_out[...] = label
    copies = []
    for block in range(1, 8):
        for index, (src, dst) in enumerate(((left, s.gather), (s.label_out, s.tags))):
            copy = pltpu.make_async_remote_copy(
                src_ref=src,
                dst_ref=dst.at[block - 1],
                send_sem=s.line_sems.at[0, index, block - 1],
                recv_sem=s.line_sems.at[1, index, block - 1],
                device_id={"member": place.xs[block // 2] * 2 + (place.core + block) % 2},
                device_id_type=MESH,
            )
            copy.start()
            copies.append(copy)
    left_label = jnp.concatenate([label[q : q + 1] for q in range(8)], axis=1)

    def against(right, tags, same):
        for q in range(8):
            s.bias[q * LANES : (q + 1) * LANES, 0:1] = column(tags, q)

        def one(index, best):
            base = pl.multiple_of(index * QUARTER, QUARTER)
            part = pl.ds(base, QUARTER)
            scores = dot_t(right[part], left[...])
            counts = s.bias[part, 0:1] == left_label
            if same:
                shape = (QUARTER, SLOTS)
                counts = counts & (iota(shape, 0) + base != iota(shape, 1))
            return jnp.maximum(best, fold(jnp.where(counts, scores, NONE)))

        start = jnp.full((8, SLOTS), NONE, jnp.float32)
        return lax.fori_loop(0, SLOTS // QUARTER, one, start)

    best = against(left, label, True)
    for copy in copies:
        copy.wait()

    def block(index, best):
        return jnp.maximum(best, against(s.gather.at[index], s.tags[index], False))

    best = jnp.max(lax.fori_loop(0, 7, block, best), axis=0, keepdims=True)
    for q in range(8):
        s.best_out[q] = best[:, q * LANES : (q + 1) * LANES]
    to_sources(place, s.best_out, s.best_in, 1, s.send_sems.at[2], s.best_sem)
    wait_for(s.best_in, s.best_sem)
    found = s.best_in[...].reshape(CELLS, LANES)
    score = sum(dot(piece, at_lane) for piece in split3(found))
    s.out[...] = jnp.maximum(jnp.sum(score * in_cell, axis=0, keepdims=True), -1.0)
    wait_sent(s)
    wait_for(s.best_in.at[pl.ds(0, CELLS - 1)], s.send_sems.at[2])


def call(kernel, name, collective, extra, embed, destination, cluster):
    rows, features = embed.shape
    bf16, f32, i32 = jnp.bfloat16, jnp.float32, jnp.int32
    vmem, dma = pltpu.VMEM, pltpu.SemaphoreType.DMA
    scratch = dict(
        dest=vmem((1, rows), i32),
        cluster=vmem((1, rows), i32),
        embed=vmem((rows, features), bf16),
        send=vmem((SLOTS, features), bf16),
        meta=vmem((CELLS, 1, LANES), f32),
        meta_in=vmem((CELLS, 1, LANES), f32),
        bias=vmem((SLOTS, LANES), f32),
        plane_sem=pltpu.SemaphoreType.REGULAR,
        load_sems=dma((3,)),
        send_sems=dma((4,)),
        recv_sems=dma((SIDE,)),
        meta_sem=dma,
        best_sem=dma,
        **extra(features),
    )
    names = ("dest_hbm", "cluster_hbm", "embed_hbm", "out", *scratch)
    return pl.pallas_call(
        functools.partial(kernel, names),
        out_shape=jax.ShapeDtypeStruct((1, rows), f32),
        in_specs=[pl.BlockSpec(memory_space=pl.ANY)] * 3,
        out_specs=pl.BlockSpec(memory_space=pltpu.VMEM),
        scratch_shapes=list(scratch.values()),
        compiler_params=pltpu.CompilerParams(
            collective_id=collective, has_side_effects=True, vmem_limit_bytes=40 * 2**20
        ),
        name=name,
    )(destination.reshape(1, rows), cluster.reshape(1, rows), embed)


def team_scratch(features):
    bf16, f32, vmem, dma = jnp.bfloat16, jnp.float32, pltpu.VMEM, pltpu.SemaphoreType.DMA
    return dict(
        left=vmem((SLOTS + LEFT_SPILL, features), bf16),
        other=vmem((SLOTS, features), bf16),
        other_spill=vmem((FORWARD, features), bf16),
        select=vmem((SIDE, FORWARD, QUARTER), bf16),
        moved=vmem((FORWARD, features), f32),
        best=vmem((SIDE, 8, QUARTER), f32),
        forward=vmem((FORWARD, features), bf16),
        label_out=vmem((16, LANES), f32),
        label_in=vmem((16, LANES), f32),
        other_bias=vmem((SLOTS, LANES), f32),
        places_out=vmem((8, 1, LANES), f32),
        places_in=vmem((CELLS, 1, LANES), f32),
        best_out=vmem((8 * ENTRY, 1, LANES), f32),
        best_in=vmem((CELLS * ENTRY, 1, LANES), f32),
        places_sem=dma,
        pair_sems=dma((2, 8)),
        spill_sems=dma((2, 3)),
    )


def general_scratch(features):
    bf16, f32, vmem, dma = jnp.bfloat16, jnp.float32, pltpu.VMEM, pltpu.SemaphoreType.DMA
    return dict(
        left=vmem((SLOTS, features), bf16),
        gather=vmem((7, SLOTS, features), bf16),
        label_out=vmem((8, LANES), f32),
        tags=vmem((7, 8, LANES), f32),
        best_out=vmem((8, 1, LANES), f32),
        best_in=vmem((CELLS, 1, LANES), f32),
        line_sems=dma((2, 2, 7)),
    )


def shards(embed, destination, cluster):
    rows = embed.shape[0]
    scores = call(team_kernel, "team_scores", 0, team_scratch, embed, destination, cluster)

    def general(*args):
        return call(general_kernel, "general_scores", 1, general_scratch, *args).reshape(rows)

    return lax.cond(
        scores[0, 0] > 4.0,
        general,
        lambda *unused: scores.reshape(rows),
        embed,
        destination,
        cluster,
    )


def solution(mesh):
    in_specs = (P(("group", "member"), None), P(("group", "member")), P(("group", "member")))
    out_specs = P(("group", "member"))
    return jax.shard_map(shards, mesh=mesh, in_specs=in_specs, out_specs=out_specs, check_vma=False)
```

```python
import functools
import types

import jax
import jax.numpy as jnp
from jax import lax
from jax.experimental import pallas as pl
from jax.experimental.pallas import tpu as pltpu
from jax.sharding import PartitionSpec as P

MESH = pl.DeviceIdType.MESH
SIDE = 4
CELLS = 64
CELL = 16
SPILL = 80
LANES = 128
QUARTER = 256
SLOTS = CELLS * CELL
FORWARD = 3 * SPILL
LEFT_SPILL = 256
NONE = -4.0
LABELS_AT = (0, 8)
ENTRY = 3
FAILED = 8.0
EMPTY = 2.0
SPILL_ORDER = (1, 0, 2)


def split3(value):
    high = value.astype(jnp.bfloat16)
    rest = value - high.astype(jnp.float32)
    mid = rest.astype(jnp.bfloat16)
    low = (rest - mid.astype(jnp.float32)).astype(jnp.bfloat16)
    return high, mid, low


def iota(shape, dim):
    return lax.broadcasted_iota(jnp.int32, shape, dim)


def dot(left, right):
    return jnp.dot(left, right, preferred_element_type=jnp.float32)


def dot_t(left, right):
    return lax.dot_general(left, right, (((1,), (1,)), ((), ())), preferred_element_type=jnp.float32)


def fold(scores):
    rows, columns = scores.shape
    return jnp.max(scores.reshape(rows // 8, 8, columns), axis=0)


def column(tags, index):
    return jnp.transpose(tags)[:, index : index + 1]


class Place:
    def __init__(self):
        group = lax.axis_index("group")
        member = lax.axis_index("member")
        y, z = group // SIDE, group % SIDE
        x, self.core = member // 2, member % 2
        self.ys = [y] + [(y + d) % SIDE for d in range(1, SIDE)]
        self.zs = [z] + [(z + d) % SIDE for d in range(1, SIDE)]
        self.xs = [x] + [(x + d) % SIDE for d in range(1, SIDE)]
        self.y, self.z, self.x = y, z, x
        self.cell = group * SIDE + x
        self.sum = (y + z + x) % SIDE
        self.sums = [self.sum] + [(self.sum + d) % SIDE for d in range(1, SIDE)]
        self.source = self.sum * 16 + group
        self.halves = [value // 2 for value in self.ys]
        self.sibling = {"group": group, "member": x * 2 + 1 - self.core}

    def at(self, dy, dz, dx):
        return {"group": self.ys[dy] * SIDE + self.zs[dz], "member": self.xs[dx] * 2 + self.core}

    def cell_at(self, dy, dz, dx):
        return (self.ys[dy] * SIDE + self.zs[dz]) * SIDE + self.xs[dx]

    def eight_at(self, dy, dz, dx):
        return self.sums[(dy + dz + dx) % SIDE] * 2 + self.halves[dy]


def offsets(phase):
    return [(dy, dz, (phase - dy - dz) % SIDE) for dy in range(SIDE) for dz in range(SIDE)]


def mixed(phase):
    pairs = sorted(enumerate(offsets(phase)), key=lambda pair: hops(pair[1]))
    return [pair for both in zip(pairs[:8], pairs[:7:-1]) for pair in both]


def hops(offset):
    return sum(min(d, SIDE - d) for d in offset)


OTHERS = sorted(
    [offset for phase in range(SIDE) for offset in offsets(phase)][1:],
    key=lambda offset: -hops(offset),
)


def wait_for(ref, sem):
    pltpu.make_async_copy(ref, ref, sem).wait()


def greet(place):
    barrier = pltpu.get_barrier_semaphore()
    plane = [(dy, dz, 0) for dy in range(SIDE) for dz in range(SIDE)][1:]
    for offset in plane + [(0, 0, d) for d in range(1, SIDE)]:
        pl.semaphore_signal(barrier, inc=1, device_id=place.at(*offset), device_id_type=MESH)
    pl.semaphore_signal(barrier, inc=1, device_id=place.sibling, device_id_type=MESH)
    return barrier


def regroup(place, s):
    load = [
        pltpu.make_async_copy(src, dst, s.load_sems.at[n])
        for n, (src, dst) in enumerate(
            ((s.dest_hbm, s.dest), (s.cluster_hbm, s.cluster), (s.embed_hbm, s.embed))
        )
    ]
    for copy in load:
        copy.start()
    barrier = greet(place)
    load[0].wait()
    load[1].wait()

    rows = s.dest.shape[1]
    team = lax.shift_right_logical(s.dest[...], 3)
    cluster = s.cluster[...]
    in_team = (iota((16, rows), 0) == team).astype(jnp.float32)
    cells = jnp.concatenate(
        [in_team * (cluster == c).astype(jnp.float32) for c in range(4)], axis=0
    )
    earlier = (iota((rows, rows), 0) < iota((rows, rows), 1)).astype(jnp.bfloat16)
    rank = jnp.sum(cells * dot(cells.astype(jnp.bfloat16), earlier), axis=0, keepdims=True)
    counts = jnp.minimum(jnp.sum(cells, axis=1, keepdims=True), float(CELL))
    over = rank >= float(CELL)
    over_team = in_team * over.astype(jnp.float32)
    order = jnp.sum(
        over_team * dot(over_team.astype(jnp.bfloat16), earlier), axis=0, keepdims=True
    )
    filled = [
        jnp.sum(in_team * counts[16 * c : 16 * c + 16], axis=0, keepdims=True) for c in range(4)
    ]
    free0 = CELL - filled[0]
    free1 = free0 + CELL - filled[1]
    free2 = free1 + CELL - filled[2]
    chip = (
        (order >= free0).astype(jnp.int32)
        + (order >= free1).astype(jnp.int32)
        + (order >= free2).astype(jnp.int32)
    )
    spot = jnp.where(
        chip == 0,
        filled[0] + order,
        jnp.where(
            chip == 1,
            filled[1] + order - free0,
            jnp.where(chip == 2, filled[2] + order - free1, filled[3] + order - free2),
        ),
    )
    chip = jnp.where(over, chip, cluster)
    spot = jnp.where(over, spot, rank).astype(jnp.int32)
    cell = team * 4 + chip
    dy = lax.rem(lax.shift_right_logical(team, 2) + (SIDE - place.y), SIDE)
    dz = lax.rem(lax.rem(team, SIDE) + (SIDE - place.z), SIDE)
    dx = lax.rem(chip + (SIDE - place.x), SIDE)
    slot = lax.rem(dy + dz + dx, SIDE) * QUARTER + (dy * SIDE + dz) * CELL + spot
    lane = spot + (place.source % 8) * CELL

    pl.semaphore_wait(barrier, 19)
    for d in range(1, SIDE):
        device = place.at(0, 0, d)
        pl.semaphore_signal(s.plane_sem, inc=1, device_id=device, device_id_type=MESH)

    load[2].wait()

    send, left = s.send, s.left

    def landing(index):
        return pl.ds(pl.multiple_of(index * CELL, CELL), CELL)

    for phase in range(SIDE):
        base = phase * QUARTER
        chosen = (iota((QUARTER, rows), 0) + base == slot).astype(jnp.bfloat16)
        values = dot(chosen, s.embed[...])
        norm = jnp.sum(values * values, axis=1, keepdims=True)
        unit = (values * lax.rsqrt(norm + 1e-06)).astype(jnp.bfloat16)
        send[base : base + QUARTER] = unit
        if phase == 0:
            pl.semaphore_wait(s.plane_sem, 3)
            pltpu.make_async_copy(
                send.at[pl.ds(0, CELL)], left.at[landing(place.source)], s.recv_sems.at[0]
            ).start()

        for count, (index, offset) in enumerate(mixed(phase)):
            if (phase, count) == LABELS_AT:
                in_cell = (iota((CELLS, rows), 0) == cell).astype(jnp.float32)
                at_lane = (iota((LANES, rows), 0) == lane).astype(jnp.bfloat16)
                labels = (in_cell * (cluster + 1).astype(jnp.float32)).astype(jnp.bfloat16)
                s.meta[...] = dot_t(labels, at_lane).reshape(CELLS, 1, LANES)
                send_labels(place, s)
            if any(offset):
                pltpu.make_async_remote_copy(
                    src_ref=send.at[landing(phase * 16 + index)],
                    dst_ref=left.at[landing(place.source)],
                    send_sem=s.send_sems.at[0],
                    recv_sem=s.recv_sems.at[phase],
                    device_id=place.at(*offset),
                    device_id_type=MESH,
                ).start()
    return in_cell, at_lane, team, cluster, chip, lane


def send_labels(place, s):
    for offset in OTHERS:
        pltpu.make_async_remote_copy(
            src_ref=s.meta.at[pl.ds(place.cell_at(*offset), 1)],
            dst_ref=s.meta_in.at[pl.ds(place.source, 1)],
            send_sem=s.send_sems.at[1],
            recv_sem=s.meta_sem,
            device_id=place.at(*offset),
            device_id_type=MESH,
        ).start()
    pltpu.make_async_copy(
        s.meta.at[pl.ds(place.cell, 1)], s.meta_in.at[pl.ds(place.source, 1)], s.meta_sem
    ).start()


def quarter(place, phase):
    if isinstance(phase, int):
        return place.sums[-phase % SIDE]
    return (place.sum + SIDE - phase) % SIDE


def rows_of(index):
    return pl.ds(pl.multiple_of(index * QUARTER, QUARTER), QUARTER)


def arrived(place, phase):
    return rows_of(quarter(place, phase))


def to_sources(place, source_ref, dest_ref, size, send_sem, recv_sem):
    for offset in OTHERS:
        pltpu.make_async_remote_copy(
            src_ref=source_ref.at[pl.ds(place.eight_at(*offset) * size, size)],
            dst_ref=dest_ref.at[pl.ds(place.cell * size, size)],
            send_sem=send_sem,
            recv_sem=recv_sem,
            device_id=place.at(*offset),
            device_id_type=MESH,
        ).start()
    pltpu.make_async_copy(
        source_ref.at[pl.ds(place.source // 8 * size, size)],
        dest_ref.at[pl.ds(place.cell * size, size)],
        recv_sem,
    ).start()


def wait_sent(s):
    sent = pl.ds(0, SLOTS - CELL)
    wait_for(s.send.at[sent], s.send_sems.at[0])
    sent = pl.ds(0, CELLS - 1)
    wait_for(s.meta.at[sent], s.send_sems.at[1])


def team_kernel(names, *refs):
    s = types.SimpleNamespace(**dict(zip(names, refs)))
    place = Place()
    in_cell, at_lane, team, cluster, chip, lane = regroup(place, s)
    left, other = s.left, s.other
    left[SLOTS + FORWARD :] = jnp.zeros((LEFT_SPILL - FORWARD, left.shape[1]), jnp.bfloat16)

    def to_pair(src, dst, index):
        copy = pltpu.make_async_remote_copy(
            src_ref=src,
            dst_ref=dst,
            send_sem=s.pair_sems.at[0, index],
            recv_sem=s.pair_sems.at[1, index],
            device_id=place.sibling,
            device_id_type=MESH,
        )
        copy.start()
        return copy

    wait_for(s.meta_in, s.meta_sem)
    label = jnp.sum(s.meta_in[...].reshape(8, 8, LANES), axis=1)
    own = (place.x + 1).astype(jnp.float32)
    below = (iota((LANES, LANES), 0) < iota((LANES, LANES), 1)).astype(jnp.bfloat16)
    hits = [
        (label == (lax.rem(place.x + d, SIDE) + 1).astype(jnp.float32)).astype(jnp.float32)
        for d in range(1, SIDE)
    ]
    hit = jnp.concatenate(hits, axis=0)
    within = dot(hit.astype(jnp.bfloat16), below)
    totals = jnp.sum(hit, axis=1, keepdims=True)
    places = jnp.full((8, LANES), -1.0, jnp.float32)
    worst = jnp.zeros((1, 1), jnp.float32)
    row, col = iota((8, 8), 0), iota((8, 8), 1)
    for d in range(3):
        total = totals[8 * d : 8 * d + 8]
        spread = jnp.broadcast_to(total, (8, 8))
        before = jnp.sum(jnp.where(row < col, spread, 0.0), axis=0, keepdims=True)
        spread = jnp.broadcast_to(before, (8, 8))
        before = jnp.sum(jnp.where(row == col, spread, 0.0), axis=1, keepdims=True)
        position = within[8 * d : 8 * d + 8] + before
        places = jnp.where(
            (hits[d] > 0.0) & (position < float(SPILL)), position + float(SPILL * d), places
        )
        worst = jnp.maximum(worst, jnp.sum(total, axis=0, keepdims=True))
    failed = jnp.broadcast_to((worst > float(SPILL)).astype(jnp.float32), (8, LANES))
    s.label_out[0:8] = label
    s.label_out[8:16] = failed
    copy_label = to_pair(s.label_out, s.label_in, 4)
    s.places_out[...] = places.reshape(8, 1, LANES)
    to_sources(place, s.places_out, s.places_in, 1, s.send_sems.at[2], s.places_sem)
    select, forward = s.select, s.forward
    for q in range(8):
        select[q // 2, :, (q % 2) * LANES : (q % 2 + 1) * LANES] = (
            iota((FORWARD, LANES), 0).astype(jnp.float32) == places[q : q + 1]
        ).astype(jnp.bfloat16)
    taken = jnp.zeros((FORWARD, 1), jnp.float32)
    for q in range(SIDE):
        taken = taken + jnp.sum(select[q].astype(jnp.float32), axis=1, keepdims=True)
    mark = jnp.where((iota((FORWARD, LANES), 1) == 0) & (taken < 0.5), EMPTY, 0.0)
    s.moved[...] = jnp.zeros(s.moved.shape, jnp.float32)
    s.moved[:, 0:LANES] = mark
    s.best[...] = jnp.full(s.best.shape, NONE, jnp.float32)

    def set_bias(ref, tags):
        for q in range(8):
            ref[q * LANES : (q + 1) * LANES, 0:1] = jnp.where(column(tags, q) == own, 0.0, NONE)

    bias, other_bias = s.bias, s.other_bias
    set_bias(bias, label)
    copy_label.wait()
    set_bias(other_bias, s.label_in[0:8])

    def block(right, right_bias, index, target, same=False):
        part = rows_of(index)
        scores = dot_t(right[part], left[rows_of(target)]) + right_bias[part, 0:1]
        if same:
            shape = (QUARTER, QUARTER)
            scores = jnp.where(iota(shape, 0) == iota(shape, 1), NONE, scores)
        s.best[target] = jnp.maximum(s.best[target], fold(scores))

    def blocks(right, right_bias, phase, same):
        last = quarter(place, phase)
        block(right, right_bias, last, last, same)

        def one(index, carry):
            first = quarter(place, index)
            block(right, right_bias, last, first)
            block(right, right_bias, first, last)
            return carry

        lax.fori_loop(0, phase, one, 0)

    shared = []
    for phase in range(SIDE):
        part = arrived(place, phase)
        wait_for(left.at[part], s.recv_sems.at[phase])
        shared.append(to_pair(left.at[part], other.at[part], phase))
        s.moved[...] += dot(select[quarter(place, phase)], left[part])
        if phase < SIDE - 1:
            blocks(left, bias, phase, True)
            if phase > 0:
                shared[phase - 1].wait()
                blocks(other, other_bias, phase - 1, False)

    to_line = []
    for d in SPILL_ORDER:
        part = slice(d * SPILL, (d + 1) * SPILL)
        forward[part] = s.moved[part].astype(jnp.bfloat16)
        copy = pltpu.make_async_remote_copy(
            src_ref=forward.at[pl.ds(d * SPILL, SPILL)],
            dst_ref=left.at[pl.ds(SLOTS + d * SPILL, SPILL)],
            send_sem=s.spill_sems.at[0, d],
            recv_sem=s.spill_sems.at[1, d],
            device_id=place.at(0, 0, d + 1),
            device_id_type=MESH,
        )
        copy.start()
        to_line.append(copy)
    blocks(left, bias, SIDE - 1, True)
    for phase in (SIDE - 2, SIDE - 1):
        shared[phase].wait()
        blocks(other, other_bias, phase, False)

    rows = cluster.shape[1]
    wait_for(s.places_in, s.places_sem)
    held = dot(s.places_in[...].reshape(CELLS, LANES).astype(jnp.bfloat16), at_lane)
    held = jnp.sum(held * in_cell, axis=0, keepdims=True).astype(jnp.int32)
    straight = chip == cluster
    entry = ENTRY * (team * 4 + cluster) + jnp.where(
        straight, 0, 1 + (held >= LANES).astype(jnp.int32)
    )
    in_entry = (iota((ENTRY * CELLS, rows), 0) == entry).astype(jnp.float32)
    spot = jnp.where(straight, lane, jnp.where(held >= LANES, held - LANES, held))
    at_spot = (iota((LANES, rows), 0) == spot).astype(jnp.bfloat16)

    spill_pair = []
    for d, copy in zip(SPILL_ORDER, to_line):
        copy.wait()
        part = pl.ds(d * SPILL, SPILL)
        spill_pair.append(
            to_pair(left.at[pl.ds(SLOTS + d * SPILL, SPILL)], s.other_spill.at[part], 5 + d)
        )

    def against(right, right_bias, best):
        return jnp.maximum(best, fold(dot_t(right[0:SLOTS], left[SLOTS:]) + right_bias[:, 0:1]))

    def against_spill(right, same):
        scores = dot_t(right, left[...]) + jnp.where(
            right[:, 0:1].astype(jnp.float32) > 1.5, NONE, 0.0
        )
        if same:
            scores = jnp.where(
                iota(scores.shape, 0) + SLOTS == iota(scores.shape, 1), NONE, scores
            )
        return fold(scores)

    best_all = against_spill(left[SLOTS : SLOTS + FORWARD], True)
    best_spill = against(other, other_bias, against(left, bias, best_all[:, SLOTS:]))
    for copy in spill_pair:
        copy.wait()
    best_all = jnp.maximum(best_all, against_spill(s.other_spill[...], False))
    best_spill = jnp.max(jnp.maximum(best_spill, best_all[:, SLOTS:]), axis=0, keepdims=True)

    failed = jnp.maximum(failed, s.label_in[8:16])[0:1]
    best_out = s.best_out
    best_main = jnp.concatenate([s.best[q] for q in range(SIDE)], axis=1)
    best_main = jnp.max(jnp.maximum(best_main, best_all[:, 0:SLOTS]), axis=0, keepdims=True)
    best_main = jnp.where(failed[0:1, 0:1] > 0.0, FAILED, best_main)
    for q in range(8):
        best_out[q * ENTRY] = best_main[:, q * LANES : (q + 1) * LANES]
        for half in range(LEFT_SPILL // LANES):
            best_out[q * ENTRY + 1 + half] = best_spill[:, half * LANES : (half + 1) * LANES]
    to_sources(place, best_out, s.best_in, ENTRY, s.send_sems.at[3], s.best_sem)
    wait_sent(s)
    wait_for(s.places_in.at[pl.ds(0, CELLS - 1)], s.send_sems.at[2])
    wait_for(s.best_in, s.best_sem)
    found = s.best_in[...].reshape(ENTRY * CELLS, LANES)
    worst = jnp.max(jnp.max(found, axis=0, keepdims=True), axis=1, keepdims=True)
    picked = sum(dot(piece, at_spot) for piece in split3(found))
    score = jnp.maximum(jnp.sum(picked * in_entry, axis=0, keepdims=True), -1.0)
    s.out[...] = jnp.where(worst > 4.0, FAILED, score)

    wait_for(s.best_in.at[pl.ds(0, ENTRY * (CELLS - 1))], s.send_sems.at[3])


def general_kernel(names, *refs):
    s = types.SimpleNamespace(**dict(zip(names, refs)))
    place = Place()
    in_cell, at_lane, *_ = regroup(place, s)
    left = s.left
    for phase in range(SIDE):
        wait_for(left.at[arrived(place, phase)], s.recv_sems.at[phase])
    wait_for(s.meta_in, s.meta_sem)
    label = jnp.sum(s.meta_in[...].reshape(8, 8, LANES), axis=1)
    s.label_out[...] = label
    copies = []
    for block in range(1, 8):
        for index, (src, dst) in enumerate(((left, s.gather), (s.label_out, s.tags))):
            copy = pltpu.make_async_remote_copy(
                src_ref=src,
                dst_ref=dst.at[block - 1],
                send_sem=s.line_sems.at[0, index, block - 1],
                recv_sem=s.line_sems.at[1, index, block - 1],
                device_id={"member": place.xs[block // 2] * 2 + (place.core + block) % 2},
                device_id_type=MESH,
            )
            copy.start()
            copies.append(copy)
    left_label = jnp.concatenate([label[q : q + 1] for q in range(8)], axis=1)

    def against(right, tags, same):
        for q in range(8):
            s.bias[q * LANES : (q + 1) * LANES, 0:1] = column(tags, q)

        def one(index, best):
            base = pl.multiple_of(index * QUARTER, QUARTER)
            part = pl.ds(base, QUARTER)
            scores = dot_t(right[part], left[...])
            counts = s.bias[part, 0:1] == left_label
            if same:
                shape = (QUARTER, SLOTS)
                counts = counts & (iota(shape, 0) + base != iota(shape, 1))
            return jnp.maximum(best, fold(jnp.where(counts, scores, NONE)))

        start = jnp.full((8, SLOTS), NONE, jnp.float32)
        return lax.fori_loop(0, SLOTS // QUARTER, one, start)

    best = against(left, label, True)
    for copy in copies:
        copy.wait()

    def block(index, best):
        return jnp.maximum(best, against(s.gather.at[index], s.tags[index], False))

    best = jnp.max(lax.fori_loop(0, 7, block, best), axis=0, keepdims=True)
    for q in range(8):
        s.best_out[q] = best[:, q * LANES : (q + 1) * LANES]
    to_sources(place, s.best_out, s.best_in, 1, s.send_sems.at[2], s.best_sem)
    wait_for(s.best_in, s.best_sem)
    found = s.best_in[...].reshape(CELLS, LANES)
    score = sum(dot(piece, at_lane) for piece in split3(found))
    s.out[...] = jnp.maximum(jnp.sum(score * in_cell, axis=0, keepdims=True), -1.0)
    wait_sent(s)
    wait_for(s.best_in.at[pl.ds(0, CELLS - 1)], s.send_sems.at[2])


def call(kernel, name, collective, extra, embed, destination, cluster):
    rows, features = embed.shape
    bf16, f32, i32 = jnp.bfloat16, jnp.float32, jnp.int32
    vmem, dma = pltpu.VMEM, pltpu.SemaphoreType.DMA
    scratch = dict(
        dest=vmem((1, rows), i32),
        cluster=vmem((1, rows), i32),
        embed=vmem((rows, features), bf16),
        send=vmem((SLOTS, features), bf16),
        meta=vmem((CELLS, 1, LANES), f32),
        meta_in=vmem((CELLS, 1, LANES), f32),
        bias=vmem((SLOTS, LANES), f32),
        plane_sem=pltpu.SemaphoreType.REGULAR,
        load_sems=dma((3,)),
        send_sems=dma((4,)),
        recv_sems=dma((SIDE,)),
        meta_sem=dma,
        best_sem=dma,
        **extra(features),
    )
    names = ("dest_hbm", "cluster_hbm", "embed_hbm", "out", *scratch)
    return pl.pallas_call(
        functools.partial(kernel, names),
        out_shape=jax.ShapeDtypeStruct((1, rows), f32),
        in_specs=[pl.BlockSpec(memory_space=pl.ANY)] * 3,
        out_specs=pl.BlockSpec(memory_space=pltpu.VMEM),
        scratch_shapes=list(scratch.values()),
        compiler_params=pltpu.CompilerParams(
            collective_id=collective, has_side_effects=True, vmem_limit_bytes=40 * 2**20
        ),
        name=name,
    )(destination.reshape(1, rows), cluster.reshape(1, rows), embed)


def team_scratch(features):
    bf16, f32, vmem, dma = jnp.bfloat16, jnp.float32, pltpu.VMEM, pltpu.SemaphoreType.DMA
    return dict(
        left=vmem((SLOTS + LEFT_SPILL, features), bf16),
        other=vmem((SLOTS, features), bf16),
        other_spill=vmem((FORWARD, features), bf16),
        select=vmem((SIDE, FORWARD, QUARTER), bf16),
        moved=vmem((FORWARD, features), f32),
        best=vmem((SIDE, 8, QUARTER), f32),
        forward=vmem((FORWARD, features), bf16),
        label_out=vmem((16, LANES), f32),
        label_in=vmem((16, LANES), f32),
        other_bias=vmem((SLOTS, LANES), f32),
        places_out=vmem((8, 1, LANES), f32),
        places_in=vmem((CELLS, 1, LANES), f32),
        best_out=vmem((8 * ENTRY, 1, LANES), f32),
        best_in=vmem((CELLS * ENTRY, 1, LANES), f32),
        places_sem=dma,
        pair_sems=dma((2, 8)),
        spill_sems=dma((2, 3)),
    )


def general_scratch(features):
    bf16, f32, vmem, dma = jnp.bfloat16, jnp.float32, pltpu.VMEM, pltpu.SemaphoreType.DMA
    return dict(
        left=vmem((SLOTS, features), bf16),
        gather=vmem((7, SLOTS, features), bf16),
        label_out=vmem((8, LANES), f32),
        tags=vmem((7, 8, LANES), f32),
        best_out=vmem((8, 1, LANES), f32),
        best_in=vmem((CELLS, 1, LANES), f32),
        line_sems=dma((2, 2, 7)),
    )


def shards(embed, destination, cluster):
    rows = embed.shape[0]
    scores = call(team_kernel, "team_scores", 0, team_scratch, embed, destination, cluster)

    def general(*args):
        return call(general_kernel, "general_scores", 1, general_scratch, *args).reshape(rows)

    return lax.cond(
        scores[0, 0] > 4.0,
        general,
        lambda *unused: scores.reshape(rows),
        embed,
        destination,
        cluster,
    )


def solution(mesh):
    in_specs = (P(("group", "member"), None), P(("group", "member")), P(("group", "member")))
    out_specs = P(("group", "member"))
    return jax.shard_map(shards, mesh=mesh, in_specs=in_specs, out_specs=out_specs, check_vma=False)
```

```python
import functools
import types

import jax
import jax.numpy as jnp
from jax import lax
from jax.experimental import pallas as pl
from jax.experimental.pallas import tpu as pltpu
from jax.sharding import PartitionSpec as P

MESH = pl.DeviceIdType.MESH
SIDE = 4
CELLS = 64
CELL = 16
SPILL = 80
LANES = 128
QUARTER = 256
SLOTS = CELLS * CELL
FORWARD = 3 * SPILL
LEFT_SPILL = 256
NONE = -4.0
META_AFTER = 0
ENTRY = 3
FAILED = 8.0
EMPTY = 2.0
SPILL_ORDER = (1, 0, 2)


def split3(value):
    high = value.astype(jnp.bfloat16)
    rest = value - high.astype(jnp.float32)
    mid = rest.astype(jnp.bfloat16)
    low = (rest - mid.astype(jnp.float32)).astype(jnp.bfloat16)
    return high, mid, low


def iota(shape, dim):
    return lax.broadcasted_iota(jnp.int32, shape, dim)


def dot(left, right):
    return jnp.dot(left, right, preferred_element_type=jnp.float32)


def dot_t(left, right):
    return lax.dot_general(left, right, (((1,), (1,)), ((), ())), preferred_element_type=jnp.float32)


def fold(scores):
    rows, columns = scores.shape
    return jnp.max(scores.reshape(rows // 8, 8, columns), axis=0)


def column(tags, index):
    return jnp.transpose(tags)[:, index : index + 1]


class Place:
    def __init__(self):
        group = lax.axis_index("group")
        member = lax.axis_index("member")
        y, z = group // SIDE, group % SIDE
        x, self.core = member // 2, member % 2
        self.ys = [y] + [(y + d) % SIDE for d in range(1, SIDE)]
        self.zs = [z] + [(z + d) % SIDE for d in range(1, SIDE)]
        self.xs = [x] + [(x + d) % SIDE for d in range(1, SIDE)]
        self.y, self.z, self.x = y, z, x
        self.cell = group * SIDE + x
        self.sum = (y + z + x) % SIDE
        self.sums = [self.sum] + [(self.sum + d) % SIDE for d in range(1, SIDE)]
        self.source = self.sum * 16 + group
        self.halves = [value // 2 for value in self.ys]
        self.sibling = {"group": group, "member": x * 2 + 1 - self.core}

    def at(self, dy, dz, dx):
        return {"group": self.ys[dy] * SIDE + self.zs[dz], "member": self.xs[dx] * 2 + self.core}

    def cell_at(self, dy, dz, dx):
        return (self.ys[dy] * SIDE + self.zs[dz]) * SIDE + self.xs[dx]

    def eight_at(self, dy, dz, dx):
        return self.sums[(dy + dz + dx) % SIDE] * 2 + self.halves[dy]


def offsets(phase):
    return [(dy, dz, (phase - dy - dz) % SIDE) for dy in range(SIDE) for dz in range(SIDE)]


def mixed(phase):
    pairs = sorted(enumerate(offsets(phase)), key=lambda pair: hops(pair[1]))
    return [pair for both in zip(pairs[:8], pairs[:7:-1]) for pair in both]


def hops(offset):
    return sum(min(d, SIDE - d) for d in offset)


OTHERS = sorted(
    [offset for phase in range(SIDE) for offset in offsets(phase)][1:],
    key=lambda offset: -hops(offset),
)


def wait_for(ref, sem):
    pltpu.make_async_copy(ref, ref, sem).wait()


def greet(place):
    barrier = pltpu.get_barrier_semaphore()
    plane = [(dy, dz, 0) for dy in range(SIDE) for dz in range(SIDE)][1:]
    for offset in plane + [(0, 0, d) for d in range(1, SIDE)]:
        pl.semaphore_signal(barrier, inc=1, device_id=place.at(*offset), device_id_type=MESH)
    pl.semaphore_signal(barrier, inc=1, device_id=place.sibling, device_id_type=MESH)
    return barrier


def regroup(place, s):
    load = [
        pltpu.make_async_copy(src, dst, s.load_sems.at[n])
        for n, (src, dst) in enumerate(
            ((s.dest_hbm, s.dest), (s.cluster_hbm, s.cluster), (s.embed_hbm, s.embed))
        )
    ]
    for copy in load:
        copy.start()
    barrier = greet(place)
    load[0].wait()
    load[1].wait()

    rows = s.dest.shape[1]
    team = lax.shift_right_logical(s.dest[...], 3)
    cluster = s.cluster[...]
    in_team = (iota((16, rows), 0) == team).astype(jnp.float32)
    cells = jnp.concatenate(
        [in_team * (cluster == c).astype(jnp.float32) for c in range(4)], axis=0
    )
    earlier = (iota((rows, rows), 0) < iota((rows, rows), 1)).astype(jnp.bfloat16)
    rank = jnp.sum(cells * dot(cells.astype(jnp.bfloat16), earlier), axis=0, keepdims=True)
    counts = jnp.minimum(jnp.sum(cells, axis=1, keepdims=True), float(CELL))
    over = rank >= float(CELL)
    over_team = in_team * over.astype(jnp.float32)
    order = jnp.sum(
        over_team * dot(over_team.astype(jnp.bfloat16), earlier), axis=0, keepdims=True
    )
    filled = [
        jnp.sum(in_team * counts[16 * c : 16 * c + 16], axis=0, keepdims=True) for c in range(4)
    ]
    free0 = CELL - filled[0]
    free1 = free0 + CELL - filled[1]
    free2 = free1 + CELL - filled[2]
    chip = (
        (order >= free0).astype(jnp.int32)
        + (order >= free1).astype(jnp.int32)
        + (order >= free2).astype(jnp.int32)
    )
    spot = jnp.where(
        chip == 0,
        filled[0] + order,
        jnp.where(
            chip == 1,
            filled[1] + order - free0,
            jnp.where(chip == 2, filled[2] + order - free1, filled[3] + order - free2),
        ),
    )
    chip = jnp.where(over, chip, cluster)
    spot = jnp.where(over, spot, rank).astype(jnp.int32)
    cell = team * 4 + chip
    dy = lax.rem(lax.shift_right_logical(team, 2) + (SIDE - place.y), SIDE)
    dz = lax.rem(lax.rem(team, SIDE) + (SIDE - place.z), SIDE)
    dx = lax.rem(chip + (SIDE - place.x), SIDE)
    slot = lax.rem(dy + dz + dx, SIDE) * QUARTER + (dy * SIDE + dz) * CELL + spot
    lane = spot + (place.source % 8) * CELL

    pl.semaphore_wait(barrier, 19)
    for d in range(1, SIDE):
        device = place.at(0, 0, d)
        pl.semaphore_signal(s.plane_sem, inc=1, device_id=device, device_id_type=MESH)

    load[2].wait()

    send, left = s.send, s.left

    def landing(index):
        return pl.ds(pl.multiple_of(index * CELL, CELL), CELL)

    for phase in range(SIDE):
        base = phase * QUARTER
        chosen = (iota((QUARTER, rows), 0) + base == slot).astype(jnp.bfloat16)
        values = dot(chosen, s.embed[...])
        norm = jnp.sum(values * values, axis=1, keepdims=True)
        unit = (values * lax.rsqrt(norm + 1e-06)).astype(jnp.bfloat16)
        send[base : base + QUARTER] = unit
        if phase == 0:
            pl.semaphore_wait(s.plane_sem, 3)
            pltpu.make_async_copy(
                send.at[pl.ds(0, CELL)], left.at[landing(place.source)], s.recv_sems.at[0]
            ).start()

        for index, offset in mixed(phase):
            if any(offset):
                pltpu.make_async_remote_copy(
                    src_ref=send.at[landing(phase * 16 + index)],
                    dst_ref=left.at[landing(place.source)],
                    send_sem=s.send_sems.at[0],
                    recv_sem=s.recv_sems.at[phase],
                    device_id=place.at(*offset),
                    device_id_type=MESH,
                ).start()
        if phase == META_AFTER:
            in_cell = (iota((CELLS, rows), 0) == cell).astype(jnp.float32)
            at_lane = (iota((LANES, rows), 0) == lane).astype(jnp.bfloat16)
            labels = (in_cell * (cluster + 1).astype(jnp.float32)).astype(jnp.bfloat16)
            s.meta[...] = dot_t(labels, at_lane).reshape(CELLS, 1, LANES)
            send_labels(place, s)
    return in_cell, at_lane, team, cluster, chip, lane


def send_labels(place, s):
    for offset in OTHERS:
        pltpu.make_async_remote_copy(
            src_ref=s.meta.at[pl.ds(place.cell_at(*offset), 1)],
            dst_ref=s.meta_in.at[pl.ds(place.source, 1)],
            send_sem=s.send_sems.at[1],
            recv_sem=s.meta_sem,
            device_id=place.at(*offset),
            device_id_type=MESH,
        ).start()
    pltpu.make_async_copy(
        s.meta.at[pl.ds(place.cell, 1)], s.meta_in.at[pl.ds(place.source, 1)], s.meta_sem
    ).start()


def quarter(place, phase):
    if isinstance(phase, int):
        return place.sums[-phase % SIDE]
    return (place.sum + SIDE - phase) % SIDE


def rows_of(index):
    return pl.ds(pl.multiple_of(index * QUARTER, QUARTER), QUARTER)


def arrived(place, phase):
    return rows_of(quarter(place, phase))


def to_sources(place, source_ref, dest_ref, size, send_sem, recv_sem):
    for offset in OTHERS:
        pltpu.make_async_remote_copy(
            src_ref=source_ref.at[pl.ds(place.eight_at(*offset) * size, size)],
            dst_ref=dest_ref.at[pl.ds(place.cell * size, size)],
            send_sem=send_sem,
            recv_sem=recv_sem,
            device_id=place.at(*offset),
            device_id_type=MESH,
        ).start()
    pltpu.make_async_copy(
        source_ref.at[pl.ds(place.source // 8 * size, size)],
        dest_ref.at[pl.ds(place.cell * size, size)],
        recv_sem,
    ).start()


def wait_sent(s):
    sent = pl.ds(0, SLOTS - CELL)
    wait_for(s.send.at[sent], s.send_sems.at[0])
    sent = pl.ds(0, CELLS - 1)
    wait_for(s.meta.at[sent], s.send_sems.at[1])


def team_kernel(names, *refs):
    s = types.SimpleNamespace(**dict(zip(names, refs)))
    place = Place()
    in_cell, at_lane, team, cluster, chip, lane = regroup(place, s)
    left, other = s.left, s.other
    left[SLOTS + FORWARD :] = jnp.zeros((LEFT_SPILL - FORWARD, left.shape[1]), jnp.bfloat16)

    def to_pair(src, dst, index):
        copy = pltpu.make_async_remote_copy(
            src_ref=src,
            dst_ref=dst,
            send_sem=s.pair_sems.at[0, index],
            recv_sem=s.pair_sems.at[1, index],
            device_id=place.sibling,
            device_id_type=MESH,
        )
        copy.start()
        return copy

    wait_for(s.meta_in, s.meta_sem)
    label = jnp.sum(s.meta_in[...].reshape(8, 8, LANES), axis=1)
    own = (place.x + 1).astype(jnp.float32)
    below = (iota((LANES, LANES), 0) < iota((LANES, LANES), 1)).astype(jnp.bfloat16)
    hits = [
        (label == (lax.rem(place.x + d, SIDE) + 1).astype(jnp.float32)).astype(jnp.float32)
        for d in range(1, SIDE)
    ]
    hit = jnp.concatenate(hits, axis=0)
    within = dot(hit.astype(jnp.bfloat16), below)
    totals = jnp.sum(hit, axis=1, keepdims=True)
    places = jnp.full((8, LANES), -1.0, jnp.float32)
    worst = jnp.zeros((1, 1), jnp.float32)
    row, col = iota((8, 8), 0), iota((8, 8), 1)
    for d in range(3):
        total = totals[8 * d : 8 * d + 8]
        spread = jnp.broadcast_to(total, (8, 8))
        before = jnp.sum(jnp.where(row < col, spread, 0.0), axis=0, keepdims=True)
        spread = jnp.broadcast_to(before, (8, 8))
        before = jnp.sum(jnp.where(row == col, spread, 0.0), axis=1, keepdims=True)
        position = within[8 * d : 8 * d + 8] + before
        places = jnp.where(
            (hits[d] > 0.0) & (position < float(SPILL)), position + float(SPILL * d), places
        )
        worst = jnp.maximum(worst, jnp.sum(total, axis=0, keepdims=True))
    failed = jnp.broadcast_to((worst > float(SPILL)).astype(jnp.float32), (8, LANES))
    s.label_out[0:8] = label
    s.label_out[8:16] = failed
    copy_label = to_pair(s.label_out, s.label_in, 4)
    s.places_out[...] = places.reshape(8, 1, LANES)
    to_sources(place, s.places_out, s.places_in, 1, s.send_sems.at[2], s.places_sem)
    select, forward = s.select, s.forward
    for q in range(8):
        select[q // 2, :, (q % 2) * LANES : (q % 2 + 1) * LANES] = (
            iota((FORWARD, LANES), 0).astype(jnp.float32) == places[q : q + 1]
        ).astype(jnp.bfloat16)
    taken = jnp.zeros((FORWARD, 1), jnp.float32)
    for q in range(SIDE):
        taken = taken + jnp.sum(select[q].astype(jnp.float32), axis=1, keepdims=True)
    mark = jnp.where((iota((FORWARD, LANES), 1) == 0) & (taken < 0.5), EMPTY, 0.0)
    s.moved[...] = jnp.zeros(s.moved.shape, jnp.float32)
    s.moved[:, 0:LANES] = mark
    s.best[...] = jnp.full(s.best.shape, NONE, jnp.float32)

    def set_bias(ref, tags):
        for q in range(8):
            ref[q * LANES : (q + 1) * LANES, 0:1] = jnp.where(column(tags, q) == own, 0.0, NONE)

    bias, other_bias = s.bias, s.other_bias
    set_bias(bias, label)
    copy_label.wait()
    set_bias(other_bias, s.label_in[0:8])

    def block(right, right_bias, index, target, same=False):
        part = rows_of(index)
        scores = dot_t(right[part], left[rows_of(target)]) + right_bias[part, 0:1]
        if same:
            shape = (QUARTER, QUARTER)
            scores = jnp.where(iota(shape, 0) == iota(shape, 1), NONE, scores)
        s.best[target] = jnp.maximum(s.best[target], fold(scores))

    def blocks(right, right_bias, phase, same):
        last = quarter(place, phase)
        block(right, right_bias, last, last, same)

        def one(index, carry):
            first = quarter(place, index)
            block(right, right_bias, last, first)
            block(right, right_bias, first, last)
            return carry

        lax.fori_loop(0, phase, one, 0)

    shared = []
    for phase in range(SIDE):
        part = arrived(place, phase)
        wait_for(left.at[part], s.recv_sems.at[phase])
        shared.append(to_pair(left.at[part], other.at[part], phase))
        s.moved[...] += dot(select[quarter(place, phase)], left[part])
        if phase < SIDE - 1:
            blocks(left, bias, phase, True)
            if phase > 0:
                shared[phase - 1].wait()
                blocks(other, other_bias, phase - 1, False)

    forward[...] = s.moved[...].astype(jnp.bfloat16)
    to_line = []
    for d in SPILL_ORDER:
        copy = pltpu.make_async_remote_copy(
            src_ref=forward.at[pl.ds(d * SPILL, SPILL)],
            dst_ref=left.at[pl.ds(SLOTS + d * SPILL, SPILL)],
            send_sem=s.spill_sems.at[0, d],
            recv_sem=s.spill_sems.at[1, d],
            device_id=place.at(0, 0, d + 1),
            device_id_type=MESH,
        )
        copy.start()
        to_line.append(copy)
    last = quarter(place, SIDE - 1)

    def last_blocks(right, right_bias, same):
        scores = dot_t(right[0:SLOTS], left[rows_of(last)]) + right_bias[:, 0:1]
        if same:
            shape = (SLOTS, QUARTER)
            scores = jnp.where(iota(shape, 0) == iota(shape, 1) + last * QUARTER, NONE, scores)
        s.best[last] = jnp.maximum(s.best[last], fold(scores))
        for phase in range(SIDE - 1):
            block(right, right_bias, last, quarter(place, phase))

    last_blocks(left, bias, True)
    shared[SIDE - 2].wait()
    blocks(other, other_bias, SIDE - 2, False)
    shared[SIDE - 1].wait()
    last_blocks(other, other_bias, False)

    rows = cluster.shape[1]
    wait_for(s.places_in, s.places_sem)
    held = dot(s.places_in[...].reshape(CELLS, LANES).astype(jnp.bfloat16), at_lane)
    held = jnp.sum(held * in_cell, axis=0, keepdims=True).astype(jnp.int32)
    straight = chip == cluster
    entry = ENTRY * (team * 4 + cluster) + jnp.where(
        straight, 0, 1 + (held >= LANES).astype(jnp.int32)
    )
    in_entry = (iota((ENTRY * CELLS, rows), 0) == entry).astype(jnp.float32)
    spot = jnp.where(straight, lane, jnp.where(held >= LANES, held - LANES, held))
    at_spot = (iota((LANES, rows), 0) == spot).astype(jnp.bfloat16)

    spill_pair = []
    for d, copy in zip(SPILL_ORDER, to_line):
        copy.wait()
        part = pl.ds(d * SPILL, SPILL)
        spill_pair.append(
            to_pair(left.at[pl.ds(SLOTS + d * SPILL, SPILL)], s.other_spill.at[part], 5 + d)
        )

    def against(right, right_bias, best):
        return jnp.maximum(best, fold(dot_t(right[0:SLOTS], left[SLOTS:]) + right_bias[:, 0:1]))

    def against_spill(right, same):
        scores = dot_t(right, left[...]) + jnp.where(
            right[:, 0:1].astype(jnp.float32) > 1.5, NONE, 0.0
        )
        if same:
            scores = jnp.where(
                iota(scores.shape, 0) + SLOTS == iota(scores.shape, 1), NONE, scores
            )
        return fold(scores)

    best_all = against_spill(left[SLOTS : SLOTS + FORWARD], True)
    best_spill = against(other, other_bias, against(left, bias, best_all[:, SLOTS:]))
    for copy in spill_pair:
        copy.wait()
    best_all = jnp.maximum(best_all, against_spill(s.other_spill[...], False))
    best_spill = jnp.max(jnp.maximum(best_spill, best_all[:, SLOTS:]), axis=0, keepdims=True)

    failed = jnp.maximum(failed, s.label_in[8:16])[0:1]
    best_out = s.best_out
    best_main = jnp.concatenate([s.best[q] for q in range(SIDE)], axis=1)
    best_main = jnp.max(jnp.maximum(best_main, best_all[:, 0:SLOTS]), axis=0, keepdims=True)
    best_main = jnp.where(failed[0:1, 0:1] > 0.0, FAILED, best_main)
    for q in range(8):
        best_out[q * ENTRY] = best_main[:, q * LANES : (q + 1) * LANES]
        for half in range(LEFT_SPILL // LANES):
            best_out[q * ENTRY + 1 + half] = best_spill[:, half * LANES : (half + 1) * LANES]
    to_sources(place, best_out, s.best_in, ENTRY, s.send_sems.at[3], s.best_sem)
    wait_sent(s)
    wait_for(s.places_in.at[pl.ds(0, CELLS - 1)], s.send_sems.at[2])
    wait_for(s.best_in, s.best_sem)
    found = s.best_in[...].reshape(ENTRY * CELLS, LANES)
    worst = jnp.max(jnp.max(found, axis=0, keepdims=True), axis=1, keepdims=True)
    picked = sum(dot(piece, at_spot) for piece in split3(found))
    score = jnp.maximum(jnp.sum(picked * in_entry, axis=0, keepdims=True), -1.0)
    s.out[...] = jnp.where(worst > 4.0, FAILED, score)

    wait_for(s.best_in.at[pl.ds(0, ENTRY * (CELLS - 1))], s.send_sems.at[3])


def general_kernel(names, *refs):
    s = types.SimpleNamespace(**dict(zip(names, refs)))
    place = Place()
    in_cell, at_lane, *_ = regroup(place, s)
    left = s.left
    for phase in range(SIDE):
        wait_for(left.at[arrived(place, phase)], s.recv_sems.at[phase])
    wait_for(s.meta_in, s.meta_sem)
    label = jnp.sum(s.meta_in[...].reshape(8, 8, LANES), axis=1)
    s.label_out[...] = label
    copies = []
    for block in range(1, 8):
        for index, (src, dst) in enumerate(((left, s.gather), (s.label_out, s.tags))):
            copy = pltpu.make_async_remote_copy(
                src_ref=src,
                dst_ref=dst.at[block - 1],
                send_sem=s.line_sems.at[0, index, block - 1],
                recv_sem=s.line_sems.at[1, index, block - 1],
                device_id={"member": place.xs[block // 2] * 2 + (place.core + block) % 2},
                device_id_type=MESH,
            )
            copy.start()
            copies.append(copy)
    left_label = jnp.concatenate([label[q : q + 1] for q in range(8)], axis=1)

    def against(right, tags, same):
        for q in range(8):
            s.bias[q * LANES : (q + 1) * LANES, 0:1] = column(tags, q)

        def one(index, best):
            base = pl.multiple_of(index * QUARTER, QUARTER)
            part = pl.ds(base, QUARTER)
            scores = dot_t(right[part], left[...])
            counts = s.bias[part, 0:1] == left_label
            if same:
                shape = (QUARTER, SLOTS)
                counts = counts & (iota(shape, 0) + base != iota(shape, 1))
            return jnp.maximum(best, fold(jnp.where(counts, scores, NONE)))

        start = jnp.full((8, SLOTS), NONE, jnp.float32)
        return lax.fori_loop(0, SLOTS // QUARTER, one, start)

    best = against(left, label, True)
    for copy in copies:
        copy.wait()

    def block(index, best):
        return jnp.maximum(best, against(s.gather.at[index], s.tags[index], False))

    best = jnp.max(lax.fori_loop(0, 7, block, best), axis=0, keepdims=True)
    for q in range(8):
        s.best_out[q] = best[:, q * LANES : (q + 1) * LANES]
    to_sources(place, s.best_out, s.best_in, 1, s.send_sems.at[2], s.best_sem)
    wait_for(s.best_in, s.best_sem)
    found = s.best_in[...].reshape(CELLS, LANES)
    score = sum(dot(piece, at_lane) for piece in split3(found))
    s.out[...] = jnp.maximum(jnp.sum(score * in_cell, axis=0, keepdims=True), -1.0)
    wait_sent(s)
    wait_for(s.best_in.at[pl.ds(0, CELLS - 1)], s.send_sems.at[2])


def call(kernel, name, collective, extra, embed, destination, cluster):
    rows, features = embed.shape
    bf16, f32, i32 = jnp.bfloat16, jnp.float32, jnp.int32
    vmem, dma = pltpu.VMEM, pltpu.SemaphoreType.DMA
    scratch = dict(
        dest=vmem((1, rows), i32),
        cluster=vmem((1, rows), i32),
        embed=vmem((rows, features), bf16),
        send=vmem((SLOTS, features), bf16),
        meta=vmem((CELLS, 1, LANES), f32),
        meta_in=vmem((CELLS, 1, LANES), f32),
        bias=vmem((SLOTS, LANES), f32),
        plane_sem=pltpu.SemaphoreType.REGULAR,
        load_sems=dma((3,)),
        send_sems=dma((4,)),
        recv_sems=dma((SIDE,)),
        meta_sem=dma,
        best_sem=dma,
        **extra(features),
    )
    names = ("dest_hbm", "cluster_hbm", "embed_hbm", "out", *scratch)
    return pl.pallas_call(
        functools.partial(kernel, names),
        out_shape=jax.ShapeDtypeStruct((1, rows), f32),
        in_specs=[pl.BlockSpec(memory_space=pl.ANY)] * 3,
        out_specs=pl.BlockSpec(memory_space=pltpu.VMEM),
        scratch_shapes=list(scratch.values()),
        compiler_params=pltpu.CompilerParams(
            collective_id=collective, has_side_effects=True, vmem_limit_bytes=40 * 2**20
        ),
        name=name,
    )(destination.reshape(1, rows), cluster.reshape(1, rows), embed)


def team_scratch(features):
    bf16, f32, vmem, dma = jnp.bfloat16, jnp.float32, pltpu.VMEM, pltpu.SemaphoreType.DMA
    return dict(
        left=vmem((SLOTS + LEFT_SPILL, features), bf16),
        other=vmem((SLOTS, features), bf16),
        other_spill=vmem((FORWARD, features), bf16),
        select=vmem((SIDE, FORWARD, QUARTER), bf16),
        moved=vmem((FORWARD, features), f32),
        best=vmem((SIDE, 8, QUARTER), f32),
        forward=vmem((FORWARD, features), bf16),
        label_out=vmem((16, LANES), f32),
        label_in=vmem((16, LANES), f32),
        other_bias=vmem((SLOTS, LANES), f32),
        places_out=vmem((8, 1, LANES), f32),
        places_in=vmem((CELLS, 1, LANES), f32),
        best_out=vmem((8 * ENTRY, 1, LANES), f32),
        best_in=vmem((CELLS * ENTRY, 1, LANES), f32),
        places_sem=dma,
        pair_sems=dma((2, 8)),
        spill_sems=dma((2, 3)),
    )


def general_scratch(features):
    bf16, f32, vmem, dma = jnp.bfloat16, jnp.float32, pltpu.VMEM, pltpu.SemaphoreType.DMA
    return dict(
        left=vmem((SLOTS, features), bf16),
        gather=vmem((7, SLOTS, features), bf16),
        label_out=vmem((8, LANES), f32),
        tags=vmem((7, 8, LANES), f32),
        best_out=vmem((8, 1, LANES), f32),
        best_in=vmem((CELLS, 1, LANES), f32),
        line_sems=dma((2, 2, 7)),
    )


def shards(embed, destination, cluster):
    rows = embed.shape[0]
    scores = call(team_kernel, "team_scores", 0, team_scratch, embed, destination, cluster)

    def general(*args):
        return call(general_kernel, "general_scores", 1, general_scratch, *args).reshape(rows)

    return lax.cond(
        scores[0, 0] > 4.0,
        general,
        lambda *unused: scores.reshape(rows),
        embed,
        destination,
        cluster,
    )


def solution(mesh):
    in_specs = (P(("group", "member"), None), P(("group", "member")), P(("group", "member")))
    out_specs = P(("group", "member"))
    return jax.shard_map(shards, mesh=mesh, in_specs=in_specs, out_specs=out_specs, check_vma=False)
```
